512 devices in a mesh: expert: 8 (over x, core), shard: 64 (over y, z).
Axes of the slice: x: 4, y: 4, z: 16, core: 2. Of those that a mesh axis runs over, the one named last changes fastest.
Arguments:
- grad: bfloat16 [32, 2048, 1408], P('expert', 'shard'), may hold values from -6 to 6
- momentum: float32 [32, 2048, 1408], P('expert', 'shard'), may hold values from -6 to 6
- owner: int32 [8, 4], P('expert'), may hold values from 0 to 3, each once within a row
Outputs:
- new_momentum: float32 [32, 2048, 1408], P('expert', 'shard')
- update: bfloat16 [32, 2048, 1408], P('expert', 'shard')
- column_residual_norms: float32 [8, 5632], P('expert', 'shard')
The draws below stay inside these ranges and needn't reach their ends.
Inputs may be any that keep to these rules, and one draw needn't show every extreme that they name: Each row of owner is a permutation of the teams 0 to 3.
All inputs are finite; a program needn't handle non-finite values.
Results may differ from the reference program's by a relative error of at most 0.017.
Values may be sent and summed in bfloat16 or wider, within the bound.
No kernel may reach another device: no remote copies, remote signals or barrier semaphores. Data moves between devices by JAX's collectives and lax.ppermute only.
A program may use at most 64 MiB of HBM per device.

```python
import math
import jax
import jax.numpy as jnp
from jax import lax

D = 2048
FF = 1408
MATS = 4
GROUPS = 8
N_EXPERT = 8


def shard_levels(stream_key, dims, pieces, least, top_value):
    def one(axis_at, shards_of):
        steps = jax.random.uniform(jax.random.fold_in(jax.random.fold_in(stream_key, 6), axis_at), (shards_of,), jnp.float32, least / len(pieces), top_value / len(pieces))
        return jnp.repeat(jnp.exp(steps), dims[axis_at] // shards_of).reshape((-1,) + (1,) * (len(dims) - axis_at - 1))

    factor_of = one(*pieces[0])
    for cut in pieces[1:]:
        factor_of = factor_of * one(*cut)
    return factor_of


def normal_values(stream_key, dims, spread, bound, pieces=(), kind=jnp.bfloat16):
    array = spread * jax.random.normal(stream_key, dims, jnp.float32)
    if pieces:
        array = array * shard_levels(stream_key, dims, pieces, -0.22, 0.18)
    return jnp.clip(array, -bound, bound).astype(kind)


def setup_inputs(seed: int = 0) -> dict:
    key_list = jax.random.split(jax.random.key(seed), 4)
    grad = normal_values(key_list[0], (GROUPS * MATS, D, FF), 1.0, 6.0, ((0, 8), (1, 64)))
    momentum = normal_values(key_list[1], (GROUPS * MATS, D, FF), 1.0, 6.0, ((0, 8), (1, 64)), jnp.float32)
    owner = jax.vmap(lambda own: jax.random.permutation(own, MATS))(jax.random.split(key_list[2], GROUPS)).reshape((GROUPS, MATS)).astype(jnp.int32)
    return dict(grad=grad, momentum=momentum, owner=owner)


DECAY = 0.95
COEF_A = 3.4445
COEF_B = -4.775
COEF_C = 2.0315
EPSILON = 1e-07

def orthogonalize(matrix):
    rounded = matrix.astype(jnp.bfloat16)
    widened = rounded.astype(jnp.float32)
    total = jnp.sqrt(jnp.sum(widened * widened))
    scale = 0.5 * math.sqrt(FF) / (total + EPSILON)
    normalized = (widened * scale).astype(jnp.bfloat16)
    flipped = normalized.T
    gram = jnp.dot(flipped, normalized, preferred_element_type=jnp.float32).astype(jnp.bfloat16)
    lifted = jnp.dot(normalized, gram, preferred_element_type=jnp.float32).astype(jnp.bfloat16)
    square = jnp.dot(flipped, lifted, preferred_element_type=jnp.float32)
    poly = (COEF_B * gram.astype(jnp.float32) + COEF_C * square).astype(jnp.bfloat16)
    ortho = COEF_A * normalized.astype(jnp.float32) + jnp.dot(normalized, poly, preferred_element_type=jnp.float32)
    ortho_b = ortho.astype(jnp.bfloat16)
    update = (math.sqrt(D) * ortho).astype(jnp.bfloat16)
    cross = jnp.dot(flipped, ortho_b, preferred_element_type=jnp.float32).astype(jnp.bfloat16)
    first = jnp.dot(normalized, cross, preferred_element_type=jnp.float32).astype(jnp.bfloat16)
    second = jnp.dot(flipped, first, preferred_element_type=jnp.float32).astype(jnp.bfloat16)
    third = jnp.dot(normalized, second, preferred_element_type=jnp.float32).astype(jnp.bfloat16)
    fourth = jnp.dot(flipped, third, preferred_element_type=jnp.float32)
    resid = COEF_A * cross.astype(jnp.float32) + COEF_B * second.astype(jnp.float32) + COEF_C * fourth - jnp.eye(FF, dtype=jnp.float32)
    return (update, jnp.sqrt(lax.optimization_barrier(jnp.sum(resid * resid, axis=0))))

def reference(grad, momentum, owner):
    new_momentum = DECAY * momentum + grad.astype(jnp.float32)
    update, norms = lax.map(orthogonalize, new_momentum)
    norms = norms.reshape(N_EXPERT, MATS, FF)
    onehot = (owner[:, :, None] == jnp.arange(MATS, dtype=jnp.int32)[None, None, :]).astype(jnp.float32)
    placed = jnp.einsum('gmt,gmf->gtf', onehot, norms)
    column_residual_norms = placed.reshape(N_EXPERT, MATS * FF)
    return (new_momentum, update, column_residual_norms)
```

```python
import math

import jax
import jax.numpy as jnp
from jax import lax
from jax.experimental import pallas as pl
from jax.experimental.pallas import tpu as pltpu
from jax.sharding import Mesh, PartitionSpec as P

DECAY = 0.95
COEF_A = 3.4445
COEF_B = -4.775
COEF_C = 2.0315
EPSILON = 1e-07

F32 = jnp.float32
BF16 = jnp.bfloat16
VMEM_LIMIT = 56 * 1024 * 1024


def momentum_kernel(owner_ref, grad_ref, momentum_ref, new_ref, payload_ref):
    new = DECAY * momentum_ref[...] + grad_ref[...].astype(F32)
    new_ref[...] = new
    payload_ref[...] = new.astype(BF16)


def momentum_step(grad, momentum, owner):
    matrices, rows, columns = grad.shape
    block = (1, rows, columns)
    return pl.pallas_call(
        momentum_kernel,
        grid_spec=pltpu.PrefetchScalarGridSpec(
            num_scalar_prefetch=1,
            grid=(matrices,),
            in_specs=[pl.BlockSpec(block, lambda m, own: (m, 0, 0))] * 2,
            out_specs=[
                pl.BlockSpec(block, lambda m, own: (m, 0, 0)),
                pl.BlockSpec(block, lambda m, own: (own[m], 0, 0)),
            ],
        ),
        out_shape=[
            jax.ShapeDtypeStruct(grad.shape, F32),
            jax.ShapeDtypeStruct(grad.shape, BF16),
        ],
        name="momentum_step",
    )(owner, grad, momentum)


def times(block, x_ref):
    return jnp.dot(block, x_ref[...], preferred_element_type=F32)


def times_transposed(block, x_ref):
    return lax.dot_general(
        block, x_ref[...], (((1,), (1,)), ((), ())), preferred_element_type=F32
    )


def ortho_kernel(width, start_ref, x_ref, update_ref, ortho_ref, scale_ref):
    total_rows, columns = x_ref.shape
    padded = ortho_ref.shape[0]
    total = jnp.zeros((16, columns), F32)
    for at in range(0, total_rows, 16):
        piece = x_ref[at : at + 16, :].astype(F32)
        total = total + piece * piece
    scale = 0.5 * math.sqrt(columns) / (jnp.sqrt(jnp.sum(total, keepdims=True)) + EPSILON)
    scale_ref[...] = jnp.broadcast_to(scale, scale_ref.shape)
    row = lax.broadcasted_iota(jnp.int32, (padded, columns), 0)
    column = lax.broadcasted_iota(jnp.int32, (padded, columns), 1)
    chosen = ((column == row + start_ref[0]) & (row < width)).astype(F32).astype(BF16)
    own = times_transposed(chosen, x_ref).astype(BF16)
    gram = ((scale * scale) * times(own, x_ref)).astype(BF16)
    lifted = (scale * times_transposed(gram, x_ref)).astype(BF16)
    square = scale * times(lifted, x_ref)
    poly = (COEF_B * gram.astype(F32) + COEF_C * square).astype(BF16)
    ortho = scale * (COEF_A * own.astype(F32) + times_transposed(poly, x_ref))
    ortho_ref[...] = ortho.astype(BF16)
    update_ref[...] = (math.sqrt(total_rows) * ortho).T[:, :width].astype(BF16)


def residual_kernel(width, start_ref, scale_ref, x_ref, ortho_ref, norms_ref):
    columns = x_ref.shape[1]
    padded = ortho_ref.shape[0]
    scale = scale_ref[0:1, 0:1]
    cross = (scale * times(ortho_ref[...], x_ref)).astype(BF16)
    first = (scale * times_transposed(cross, x_ref)).astype(BF16)
    second = (scale * times(first, x_ref)).astype(BF16)
    third = (scale * times_transposed(second, x_ref)).astype(BF16)
    fourth = scale * times(third, x_ref)
    row = lax.broadcasted_iota(jnp.int32, (padded, columns), 0)
    column = lax.broadcasted_iota(jnp.int32, (padded, columns), 1)
    identity = (column == row + start_ref[0]).astype(F32)
    resid = (
        COEF_A * cross.astype(F32) + COEF_B * second.astype(F32) + COEF_C * fourth - identity
    )
    norms_ref[...] = jnp.sqrt(jnp.sum(resid * resid, axis=1, keepdims=True))


def regroup_kernel(width, owner_ref, returned_ref, update_ref):
    for at in range(returned_ref.shape[1]):
        update_ref[0, :, at * width : (at + 1) * width] = returned_ref[0, at]


def regroup(returned, owner):
    matrices, members, rows, width = returned.shape
    return pl.pallas_call(
        lambda *refs: regroup_kernel(width, *refs),
        grid_spec=pltpu.PrefetchScalarGridSpec(
            num_scalar_prefetch=1,
            grid=(matrices,),
            in_specs=[
                pl.BlockSpec((1, members, rows, width), lambda m, own: (own[m], 0, 0, 0))
            ],
            out_specs=pl.BlockSpec((1, rows, members * width), lambda m, own: (m, 0, 0)),
        ),
        out_shape=jax.ShapeDtypeStruct((matrices, rows, members * width), BF16),
        name="regroup",
    )(owner, returned)


def on_device(grad, momentum, owner):
    matrices, rows, columns = grad.shape
    members = lax.axis_size("z")
    width = columns // members
    total_rows = rows * matrices * members
    padded = -(-width // 16) * 16
    owner = owner.reshape(matrices)
    new_momentum, payload = momentum_step(grad, momentum, owner)
    mine = lax.all_to_all(payload, "y", split_axis=0, concat_axis=0, tiled=True)
    whole = lax.all_gather(mine.reshape(matrices * rows, columns), "z", axis=0, tiled=True)
    start = (lax.axis_index("z") * width).astype(jnp.int32).reshape(1)
    smem = pl.BlockSpec(memory_space=pltpu.SMEM)
    vmem = pl.BlockSpec(memory_space=pltpu.VMEM)
    flops = 2 * padded * total_rows * columns
    update, ortho, scale = pl.pallas_call(
        lambda *refs: ortho_kernel(width, *refs),
        in_specs=[smem, vmem],
        out_specs=[vmem, vmem, vmem],
        out_shape=[
            jax.ShapeDtypeStruct((total_rows, width), BF16),
            jax.ShapeDtypeStruct((padded, total_rows), BF16),
            jax.ShapeDtypeStruct((8, 128), F32),
        ],
        compiler_params=pltpu.CompilerParams(vmem_limit_bytes=VMEM_LIMIT),
        cost_estimate=pl.CostEstimate(
            flops=5 * flops, bytes_accessed=2 * total_rows * columns, transcendentals=0
        ),
        name="ortho",
    )(start, whole)
    returned = lax.all_to_all(
        update.reshape(members, matrices, rows, width).swapaxes(0, 1).reshape(-1, rows, width),
        ("y", "z"),
        split_axis=0,
        concat_axis=0,
        tiled=True,
    )
    norms = pl.pallas_call(
        lambda *refs: residual_kernel(width, *refs),
        in_specs=[smem, vmem, vmem, vmem],
        out_specs=vmem,
        out_shape=jax.ShapeDtypeStruct((padded, 1), F32),
        compiler_params=pltpu.CompilerParams(vmem_limit_bytes=VMEM_LIMIT),
        cost_estimate=pl.CostEstimate(
            flops=5 * flops, bytes_accessed=2 * total_rows * columns, transcendentals=0
        ),
        name="residual",
    )(start, scale, whole, ortho)
    out_update = regroup(returned.reshape(matrices, members, rows, width), owner)
    return new_momentum, out_update, norms[:width, 0][None, :]


def solution(mesh):
    experts, shards = mesh.devices.shape
    split = Mesh(mesh.devices.reshape(experts // 2, 2, 4, shards // 4), ("x", "core", "y", "z"))
    groups, rows = ("x", "core"), ("y", "z")
    return jax.shard_map(
        on_device,
        mesh=split,
        in_specs=(P(groups, rows, None), P(groups, rows, None), P(groups, None)),
        out_specs=(P(groups, rows, None), P(groups, rows, None), P(groups, rows)),
        check_vma=False,
    )
```

```python
import math

import jax
import jax.numpy as jnp
from jax import lax
from jax.experimental import pallas as pl
from jax.experimental.pallas import tpu as pltpu
from jax.sharding import Mesh, PartitionSpec as P

DECAY = 0.95
COEF_A = 3.4445
COEF_B = -4.775
COEF_C = 2.0315
EPSILON = 1e-07

F32 = jnp.float32
BF16 = jnp.bfloat16
VMEM_LIMIT = 56 * 1024 * 1024
LANES = 128
Y_OFFSETS = (0, 3, 1, 2)


def momentum_kernel(grad_ref, momentum_ref, new_ref, payload_ref):
    new = DECAY * momentum_ref[...] + grad_ref[...].astype(F32)
    new_ref[...] = new
    rounded = new.astype(BF16)
    half = payload_ref.shape[2]
    payload_ref[0] = rounded[:, :half]
    payload_ref[1] = rounded[:, half:]


def momentum_step(grad, momentum):
    matrices, rows, columns = grad.shape
    vmem = pl.BlockSpec(memory_space=pltpu.VMEM)
    return pl.pallas_call(
        momentum_kernel,
        in_specs=[vmem, vmem],
        out_specs=[vmem, vmem],
        out_shape=[
            jax.ShapeDtypeStruct(grad.shape, F32),
            jax.ShapeDtypeStruct((2, matrices, rows // 2, columns), BF16),
        ],
        compiler_params=pltpu.CompilerParams(vmem_limit_bytes=VMEM_LIMIT),
        name="momentum_step",
    )(grad, momentum)


def times(block, x_ref):
    return jnp.dot(block, x_ref[...], preferred_element_type=F32)


def times_transposed(block, x_ref):
    return lax.dot_general(
        block, x_ref[...], (((1,), (1,)), ((), ())), preferred_element_type=F32
    )


def products_kernel(width, padded, place_ref, *refs):
    sections = refs[:16]
    slots_ref, x_ref, sems = refs[16:]
    core, y, b = place_ref[0], place_ref[1], place_ref[2]
    total_rows, columns = x_ref.shape
    section_rows = total_rows // 16
    copies = [
        pltpu.make_async_copy(
            ref, x_ref.at[pl.ds(at * section_rows, section_rows)], sems.at[at]
        )
        for at, ref in enumerate(sections)
    ]
    for copy in copies:
        copy.start()
    total = jnp.zeros((16, columns), F32)
    for at, copy in enumerate(copies):
        copy.wait()
        for low in range(at * section_rows, (at + 1) * section_rows, 16):
            piece = x_ref[low : low + 16, :].astype(F32)
            total = total + piece * piece
    scale = 0.5 * math.sqrt(columns) / (jnp.sqrt(jnp.sum(total, keepdims=True)) + EPSILON)
    start = width * (core * 8 + y * 2 + b)
    row = lax.broadcasted_iota(jnp.int32, (padded, columns), 0)
    column = lax.broadcasted_iota(jnp.int32, (padded, columns), 1)
    identity = ((column == row + start) & (row < width)).astype(F32)
    own = times_transposed(identity.astype(BF16), x_ref).astype(BF16)
    gram = ((scale * scale) * times(own, x_ref)).astype(BF16)
    lifted = (scale * times_transposed(gram, x_ref)).astype(BF16)
    square = scale * times(lifted, x_ref)
    poly = (COEF_B * gram.astype(F32) + COEF_C * square).astype(BF16)
    ortho = scale * (COEF_A * own.astype(F32) + times_transposed(poly, x_ref))
    cross = (scale * times(ortho.astype(BF16), x_ref)).astype(BF16)
    first = (scale * times_transposed(cross, x_ref)).astype(BF16)
    second = (scale * times(first, x_ref)).astype(BF16)
    third = (scale * times_transposed(second, x_ref)).astype(BF16)
    fourth = scale * times(third, x_ref)
    resid = (
        COEF_A * cross.astype(F32) + COEF_B * second.astype(F32) + COEF_C * fourth - identity
    )
    norms = jnp.sqrt(jnp.sum(resid * resid, axis=1, keepdims=True))
    high = norms.astype(BF16).astype(F32)
    low = norms - high
    lane = lax.broadcasted_iota(jnp.int32, (32, LANES), 1)
    extra = jnp.zeros((32, LANES), F32)
    for part in range(3):
        cut = slice(32 * part, 32 * part + 32)
        extra = jnp.where(lane == width + part, high[cut], extra)
        extra = jnp.where(lane == width + 3 + part, low[cut], extra)
    update = math.sqrt(total_rows) * ortho
    below = jnp.zeros((LANES - padded, section_rows), F32)

    def turned(at):
        piece = update[:, at * section_rows : (at + 1) * section_rows]
        return jnp.concatenate([piece, below], axis=0).T.reshape(16, 8, LANES)

    for core_step in range(2):
        half = core ^ core_step
        place = pl.ds(pl.multiple_of(half * 16, 16), 16)
        tail = jnp.where(half == 0, extra[:16], extra[16:])
        for step, offset in enumerate(Y_OFFSETS):
            mine = turned((core_step * 4 + step) * 2)
            other = turned((core_step * 4 + step) * 2 + 1)
            ordered = jnp.concatenate(
                [jnp.where(b == 0, mine, other), jnp.where(b == 0, other, mine)], axis=1
            )
            slots_ref[:, (y + offset) % 4, place, :] = (ordered + tail[None]).astype(BF16)


def products(sections, place, width, padded):
    section_rows, columns = sections[0].shape
    total_rows = 16 * section_rows
    return pl.pallas_call(
        lambda *refs: products_kernel(width, padded, *refs),
        in_specs=[pl.BlockSpec(memory_space=pltpu.SMEM)]
        + [pl.BlockSpec(memory_space=pl.ANY)] * 16,
        out_specs=pl.BlockSpec(memory_space=pltpu.VMEM),
        out_shape=jax.ShapeDtypeStruct((16, 4, 32, LANES), BF16),
        scratch_shapes=[
            pltpu.VMEM((total_rows, columns), BF16),
            pltpu.SemaphoreType.DMA((16,)),
        ],
        compiler_params=pltpu.CompilerParams(vmem_limit_bytes=VMEM_LIMIT),
        cost_estimate=pl.CostEstimate(
            flops=20 * padded * total_rows * columns,
            bytes_accessed=2 * total_rows * columns,
            transcendentals=0,
        ),
        name="products",
    )(place, *sections)


def regroup_kernel(width, place_ref, owner_ref, returned_ref, update_ref, norms_ref):
    y, z = place_ref[1], place_ref[3]
    matrices = update_ref.shape[0]
    for m in range(matrices):
        for at in range(16):
            core, source_y, b = at // 8, (at // 2) % 4, at % 2
            update_ref[m, :, at * width : (at + 1) * width] = returned_ref[
                core, m, b, source_y, :, :width
            ]

        @pl.when(owner_ref[m] == y)
        def _():
            slot = returned_ref[z // 8, m, z % 2, (z // 2) % 4].astype(F32).T
            for part in range(3):
                value = slot[width + part : width + part + 1]
                value = value + slot[width + 3 + part : width + 4 + part]
                size = min(32, width - 32 * part)
                norms_ref[:, 32 * part : 32 * part + size] = value[:, :size]


def regroup(returned, place, owner, width):
    matrices, rows = returned.shape[1], returned.shape[4]
    smem = pl.BlockSpec(memory_space=pltpu.SMEM)
    vmem = pl.BlockSpec(memory_space=pltpu.VMEM)
    return pl.pallas_call(
        lambda *refs: regroup_kernel(width, *refs),
        in_specs=[smem, smem, vmem],
        out_specs=[vmem, vmem],
        out_shape=[
            jax.ShapeDtypeStruct((matrices, rows, 16 * width), BF16),
            jax.ShapeDtypeStruct((1, width), F32),
        ],
        compiler_params=pltpu.CompilerParams(vmem_limit_bytes=VMEM_LIMIT),
        name="regroup",
    )(place, owner, returned)


def on_device(grad, momentum, owner):
    matrices, rows, columns = grad.shape
    width = columns // 16
    padded = -(-width // 16) * 16
    core, y, z = lax.axis_index("core"), lax.axis_index("y"), lax.axis_index("z")
    place = jnp.stack([core, y, z % 2, z]).astype(jnp.int32)
    up = [(i, (i + 1) % 4) for i in range(4)]
    down = [((i + 1) % 4, i) for i in range(4)]

    new_momentum, payload = momentum_step(grad, momentum)
    halves = lax.all_to_all(payload, "core", split_axis=0, concat_axis=0, tiled=True)
    mine = lax.all_to_all(
        halves.reshape(16, rows // 4, columns), "z", split_axis=0, concat_axis=0, tiled=True
    ).reshape(-1, columns)
    other = lax.ppermute(mine, "z", [(i, i ^ 1) for i in range(16)])
    mine_left = lax.ppermute(mine, "y", up)
    mine_right = lax.ppermute(mine, "y", down)
    other_left = lax.ppermute(other, "y", up)
    other_right = lax.ppermute(other, "y", down)
    mine_far = lax.ppermute(mine_left, "y", up)
    other_far = lax.ppermute(other_right, "y", down)
    near = [mine, other, mine_left, other_left, mine_right, other_right, mine_far, other_far]
    swapped = [lax.ppermute(part, "core", [(0, 1), (1, 0)]) for part in near]

    slots = products(near + swapped, place, width, padded)
    returned = lax.all_to_all(
        slots.reshape(64, rows, LANES), ("z", "y"), split_axis=0, concat_axis=0, tiled=True
    )
    returned = lax.all_to_all(
        returned.reshape(2, -1, rows, LANES), "core", split_axis=0, concat_axis=0, tiled=True
    )
    returned = returned.reshape(2, matrices, 2, 4, rows, LANES)
    out_update, norms = regroup(returned, place, owner.reshape(matrices), width)
    return new_momentum, out_update, norms


def solution(mesh):
    experts, shards = mesh.devices.shape
    split = Mesh(mesh.devices.reshape(experts // 2, 2, 4, shards // 4), ("x", "core", "y", "z"))
    groups, rows = ("x", "core"), ("y", "z")
    return jax.shard_map(
        on_device,
        mesh=split,
        in_specs=(P(groups, rows, None), P(groups, rows, None), P(groups, None)),
        out_specs=(P(groups, rows, None), P(groups, rows, None), P(groups, rows)),
        check_vma=False,
    )
```

```python
import math

import jax
import jax.numpy as jnp
from jax import lax
from jax.experimental import pallas as pl
from jax.experimental.pallas import tpu as pltpu
from jax.sharding import Mesh, PartitionSpec as P

DECAY = 0.95
COEF_A = 3.4445
COEF_B = -4.775
COEF_C = 2.0315
EPSILON = 1e-07

F32 = jnp.float32
BF16 = jnp.bfloat16
VMEM_LIMIT = 56 * 1024 * 1024
LANES = 128
SECTION_SIZES = (1, 1, 1, 1, 2, 2, 2, 2, 2, 2)
SLOT_ROWS = 24
HIGH_LANE = 96
LOW_LANE = 112


def momentum_kernel(grad_ref, momentum_ref, new_ref, payload_ref):
    new = DECAY * momentum_ref[...] + grad_ref[...].astype(F32)
    new_ref[...] = new
    rounded = new.astype(BF16)
    half = payload_ref.shape[2]
    payload_ref[0] = rounded[:, :half]
    payload_ref[1] = rounded[:, half:]


def momentum_step(grad, momentum):
    matrices, rows, columns = grad.shape
    vmem = pl.BlockSpec(memory_space=pltpu.VMEM)
    return pl.pallas_call(
        momentum_kernel,
        in_specs=[vmem, vmem],
        out_specs=[vmem, vmem],
        out_shape=[
            jax.ShapeDtypeStruct(grad.shape, F32),
            jax.ShapeDtypeStruct((2, matrices, rows // 2, columns), BF16),
        ],
        compiler_params=pltpu.CompilerParams(vmem_limit_bytes=VMEM_LIMIT),
        name="momentum_step",
    )(grad, momentum)


def times(block, x_ref):
    return jnp.dot(block, x_ref[...], preferred_element_type=F32)


def times_transposed(block, x_ref):
    return lax.dot_general(
        block, x_ref[...], (((1,), (1,)), ((), ())), preferred_element_type=F32
    )


def products_kernel(width, padded, place_ref, *refs):
    count = len(SECTION_SIZES)
    sections = refs[:count]
    slots_ref, x_ref, sems = refs[count:]
    core, y, b = place_ref[0], place_ref[1], place_ref[2]
    total_rows, columns = x_ref.shape
    section_rows = total_rows // 16
    copies = []
    at = 0
    for ref, size in zip(sections, SECTION_SIZES):
        rows = pl.ds(at * section_rows, size * section_rows)
        copies.append(pltpu.make_async_copy(ref, x_ref.at[rows], sems.at[len(copies)]))
        at += size
    for copy in copies:
        copy.start()
    total = jnp.zeros((16, columns), F32)
    at = 0
    for copy, size in zip(copies, SECTION_SIZES):
        copy.wait()
        for low in range(at * section_rows, (at + size) * section_rows, 16):
            piece = x_ref[low : low + 16, :].astype(F32)
            total = total + piece * piece
        at += size
    scale = 0.5 * math.sqrt(columns) / (jnp.sqrt(jnp.sum(total, keepdims=True)) + EPSILON)
    start = width * (core * 8 + y * 2 + b)
    row = lax.broadcasted_iota(jnp.int32, (padded, columns), 0)
    column = lax.broadcasted_iota(jnp.int32, (padded, columns), 1)
    identity = ((column == row + start) & (row < width)).astype(F32)
    own = times_transposed(identity.astype(BF16), x_ref).astype(BF16)
    gram = ((scale * scale) * times(own, x_ref)).astype(BF16)
    lifted = (scale * times_transposed(gram, x_ref)).astype(BF16)
    square = scale * times(lifted, x_ref)
    poly = (COEF_B * gram.astype(F32) + COEF_C * square).astype(BF16)
    ortho = scale * (COEF_A * own.astype(F32) + times_transposed(poly, x_ref))
    cross = (scale * times(ortho.astype(BF16), x_ref)).astype(BF16)
    first = (scale * times_transposed(cross, x_ref)).astype(BF16)
    second = (scale * times(first, x_ref)).astype(BF16)
    third = (scale * times_transposed(second, x_ref)).astype(BF16)
    fourth = scale * times(third, x_ref)
    resid = (
        COEF_A * cross.astype(F32) + COEF_B * second.astype(F32) + COEF_C * fourth - identity
    )
    norms = jnp.sqrt(jnp.sum(resid * resid, axis=1, keepdims=True))
    high = norms.astype(BF16).astype(F32)
    low = norms - high
    lane = lax.broadcasted_iota(jnp.int32, (8, LANES), 1)
    extra = jnp.zeros((8, LANES), F32)
    for part in range(width // 8):
        cut = slice(8 * part, 8 * part + 8)
        extra = jnp.where(lane == HIGH_LANE + part, high[cut], extra)
        extra = jnp.where(lane == LOW_LANE + part, low[cut], extra)
    update = math.sqrt(total_rows) * ortho
    below = jnp.zeros((LANES - padded, section_rows), F32)
    spare = lax.broadcasted_iota(jnp.int32, (16, 8, LANES), 2) >= width

    def turned(at):
        piece = update[:, at * section_rows : (at + 1) * section_rows]
        return jnp.concatenate([piece, below], axis=0).T.reshape(16, 8, LANES)

    def spill(rows, by):
        return jnp.where(spare, pltpu.roll(rows, by, 2), 0.0)

    for offset, flip, mine, other in (
        (0, 0, (0, 2), (1, 3)),
        (3 - 2 * core, 0, (4, 6), (5, 7)),
        (1 + 2 * core, 0, (9, 11), (8, 10)),
        (2, core, (12, 15), (13, 14)),
    ):
        swap = (flip ^ b) == 1
        parts = []
        for pair in (mine, other):
            one, two = turned(pair[0]), turned(pair[1])
            parts.append((jnp.where(swap, two, one), jnp.where(swap, one, two)))
        tiles = [jnp.where(core == 0, parts[0][i], parts[1][i]) for i in range(2)]
        tiles += [jnp.where(core == 0, parts[1][i], parts[0][i]) for i in range(2)]
        last = tiles[3]
        packed = jnp.concatenate(
            [
                tiles[0] + spill(last, 88),
                tiles[1] + spill(last, 48),
                tiles[2] + spill(last, 8) + extra,
            ],
            axis=1,
        )
        slots_ref[:, (y + offset) % 4] = packed.astype(BF16)


def products(sections, place, width, padded):
    columns = sections[0].shape[1]
    total_rows = sum(part.shape[0] for part in sections)
    return pl.pallas_call(
        lambda *refs: products_kernel(width, padded, *refs),
        in_specs=[pl.BlockSpec(memory_space=pltpu.SMEM)]
        + [pl.BlockSpec(memory_space=pl.ANY)] * len(sections),
        out_specs=pl.BlockSpec(memory_space=pltpu.VMEM),
        out_shape=jax.ShapeDtypeStruct((16, 4, SLOT_ROWS, LANES), BF16),
        scratch_shapes=[
            pltpu.VMEM((total_rows, columns), BF16),
            pltpu.SemaphoreType.DMA((len(sections),)),
        ],
        compiler_params=pltpu.CompilerParams(vmem_limit_bytes=VMEM_LIMIT),
        cost_estimate=pl.CostEstimate(
            flops=20 * padded * total_rows * columns,
            bytes_accessed=2 * total_rows * columns,
            transcendentals=0,
        ),
        name="products",
    )(place, *sections)


def regroup_kernel(width, place_ref, owner_ref, returned_ref, update_ref, norms_ref):
    y, z = place_ref[1], place_ref[3]
    matrices = update_ref.shape[0]
    lane = lax.broadcasted_iota(jnp.int32, (8, LANES), 1)
    for m in range(matrices):
        for at in range(16):
            core, source_y, b = at // 8, (at // 2) % 4, at % 2
            slot = returned_ref[core, m, b, source_y].astype(F32)
            last = jnp.where(
                lane < 40,
                pltpu.roll(slot[:8], 40, 1),
                jnp.where(lane < 80, pltpu.roll(slot[8:16], 80, 1), pltpu.roll(slot[16:], 120, 1)),
            )
            rows = jnp.concatenate([slot, last], axis=0).astype(BF16)
            update_ref[m, :, at * width : (at + 1) * width] = rows[:, :width]

        @pl.when(owner_ref[m] == y)
        def _():
            slot = returned_ref[z // 8, m, z % 2, (z // 2) % 4].astype(F32)
            turned = jnp.concatenate([slot[16:], slot], axis=0).T
            for part in range(width // 8):
                value = turned[HIGH_LANE + part : HIGH_LANE + part + 1, :8]
                value = value + turned[LOW_LANE + part : LOW_LANE + part + 1, :8]
                norms_ref[:, 8 * part : 8 * part + 8] = value


def regroup(returned, place, owner, width):
    matrices = returned.shape[1]
    smem = pl.BlockSpec(memory_space=pltpu.SMEM)
    vmem = pl.BlockSpec(memory_space=pltpu.VMEM)
    return pl.pallas_call(
        lambda *refs: regroup_kernel(width, *refs),
        in_specs=[smem, smem, vmem],
        out_specs=[vmem, vmem],
        out_shape=[
            jax.ShapeDtypeStruct((matrices, SLOT_ROWS + 8, 16 * width), BF16),
            jax.ShapeDtypeStruct((1, width), F32),
        ],
        compiler_params=pltpu.CompilerParams(vmem_limit_bytes=VMEM_LIMIT),
        name="regroup",
    )(place, owner, returned)


def on_device(grad, momentum, owner):
    matrices, rows, columns = grad.shape
    width = columns // 16
    padded = -(-width // 16) * 16
    core, y, z = lax.axis_index("core"), lax.axis_index("y"), lax.axis_index("z")
    place = jnp.stack([core, y, z % 2, z]).astype(jnp.int32)
    ring = [(i, (i + 1) % 4) for i in range(4)] + [(4 + i, 4 + (i + 3) % 4) for i in range(4)]
    swap = [(0, 1), (1, 0)]

    new_momentum, payload = momentum_step(grad, momentum)
    halves = lax.all_to_all(payload, "core", split_axis=0, concat_axis=0, tiled=True)
    mine = lax.all_to_all(
        halves.reshape(16, rows // 4, columns), "z", split_axis=0, concat_axis=0, tiled=True
    ).reshape(-1, columns)
    other = lax.ppermute(mine, "z", [(i, i ^ 1) for i in range(16)])
    mine_swapped = lax.ppermute(mine, "core", swap)
    both_mine = jnp.concatenate([mine, mine_swapped], axis=0)
    near_mine = lax.ppermute(both_mine, ("core", "y"), ring)
    other_swapped = lax.ppermute(other, "core", swap)
    both_other = jnp.concatenate([other, other_swapped], axis=0)
    near_other = lax.ppermute(both_other, ("core", "y"), ring)
    far = lax.ppermute(jnp.where(core == 0, near_mine, near_other), ("core", "y"), ring)
    near_mine_swapped = lax.ppermute(near_mine, "core", swap)
    near_other_swapped = lax.ppermute(near_other, "core", swap)
    far_swapped = lax.ppermute(far, "core", swap)
    sections = [mine, mine_swapped, other, other_swapped, near_mine, near_other]
    sections += [near_mine_swapped, near_other_swapped, far, far_swapped]

    slots = products(sections, place, width, padded)
    returned = lax.all_to_all(
        slots.reshape(64, SLOT_ROWS, LANES), ("z", "y"), split_axis=0, concat_axis=0, tiled=True
    )
    returned = lax.all_to_all(
        returned.reshape(2, -1, SLOT_ROWS, LANES), "core", split_axis=0, concat_axis=0, tiled=True
    )
    returned = returned.reshape(2, matrices, 2, 4, SLOT_ROWS, LANES)
    out_update, norms = regroup(returned, place, owner.reshape(matrices), width)
    return new_momentum, out_update, norms


def solution(mesh):
    experts, shards = mesh.devices.shape
    split = Mesh(mesh.devices.reshape(experts // 2, 2, 4, shards // 4), ("x", "core", "y", "z"))
    groups, rows = ("x", "core"), ("y", "z")
    return jax.shard_map(
        on_device,
        mesh=split,
        in_specs=(P(groups, rows, None), P(groups, rows, None), P(groups, None)),
        out_specs=(P(groups, rows, None), P(groups, rows, None), P(groups, rows)),
        check_vma=False,
    )
```

```python
import math

import jax
import jax.numpy as jnp
from jax import lax
from jax.experimental import pallas as pl
from jax.experimental.pallas import tpu as pltpu
from jax.sharding import Mesh, PartitionSpec as P

DECAY = 0.95
COEF_A = 3.4445
COEF_B = -4.775
COEF_C = 2.0315
EPSILON = 1e-07

F32 = jnp.float32
BF16 = jnp.bfloat16
VMEM_LIMIT = 40 * 1024 * 1024
LANES = 128
Y_OFFSETS = (0, 3, 1, 2)
SECTION_SIZES = (2, 4, 2, 2, 4, 2)
SLOT_ROWS = 24
HIGH_LANE = 96
LOW_LANE = 112


def momentum_kernel(grad_ref, momentum_ref, new_ref, payload_ref):
    new = DECAY * momentum_ref[...] + grad_ref[...].astype(F32)
    new_ref[...] = new
    rounded = new.astype(BF16)
    half = payload_ref.shape[2]
    payload_ref[0] = rounded[:, :half]
    payload_ref[1] = rounded[:, half:]


def momentum_step(grad, momentum):
    matrices, rows, columns = grad.shape
    vmem = pl.BlockSpec(memory_space=pltpu.VMEM)
    return pl.pallas_call(
        momentum_kernel,
        in_specs=[vmem, vmem],
        out_specs=[vmem, vmem],
        out_shape=[
            jax.ShapeDtypeStruct(grad.shape, F32),
            jax.ShapeDtypeStruct((2, matrices, rows // 2, columns), BF16),
        ],
        compiler_params=pltpu.CompilerParams(vmem_limit_bytes=VMEM_LIMIT),
        name="momentum_step",
    )(grad, momentum)


def times(block, x_ref):
    return jnp.dot(block, x_ref[...], preferred_element_type=F32)


def times_transposed(block, x_ref):
    return lax.dot_general(
        block, x_ref[...], (((1,), (1,)), ((), ())), preferred_element_type=F32
    )


def products_kernel(width, padded, place_ref, *refs):
    count = len(SECTION_SIZES)
    sections = refs[:count]
    slots_ref, x_ref, sems = refs[count:]
    core, y, b = place_ref[0], place_ref[1], place_ref[2]
    total_rows, columns = x_ref.shape
    section_rows = total_rows // 16
    copies = []
    at = 0
    for ref, size in zip(sections, SECTION_SIZES):
        rows = pl.ds(at * section_rows, size * section_rows)
        copies.append(pltpu.make_async_copy(ref, x_ref.at[rows], sems.at[len(copies)]))
        at += size
    for copy in copies:
        copy.start()
    total = jnp.zeros((16, columns), F32)
    at = 0
    for copy, size in zip(copies, SECTION_SIZES):
        copy.wait()
        for low in range(at * section_rows, (at + size) * section_rows, 16):
            piece = x_ref[low : low + 16, :].astype(F32)
            total = total + piece * piece
        at += size
    scale = 0.5 * math.sqrt(columns) / (jnp.sqrt(jnp.sum(total, keepdims=True)) + EPSILON)
    start = width * (core * 8 + y * 2 + b)
    row = lax.broadcasted_iota(jnp.int32, (padded, columns), 0)
    column = lax.broadcasted_iota(jnp.int32, (padded, columns), 1)
    identity = ((column == row + start) & (row < width)).astype(F32)
    own = times_transposed(identity.astype(BF16), x_ref).astype(BF16)
    gram = ((scale * scale) * times(own, x_ref)).astype(BF16)
    lifted = (scale * times_transposed(gram, x_ref)).astype(BF16)
    square = scale * times(lifted, x_ref)
    poly = (COEF_B * gram.astype(F32) + COEF_C * square).astype(BF16)
    ortho = scale * (COEF_A * own.astype(F32) + times_transposed(poly, x_ref))
    cross = (scale * times(ortho.astype(BF16), x_ref)).astype(BF16)
    first = (scale * times_transposed(cross, x_ref)).astype(BF16)
    second = (scale * times(first, x_ref)).astype(BF16)
    third = (scale * times_transposed(second, x_ref)).astype(BF16)
    fourth = scale * times(third, x_ref)
    resid = (
        COEF_A * cross.astype(F32) + COEF_B * second.astype(F32) + COEF_C * fourth - identity
    )
    norms = jnp.sqrt(jnp.sum(resid * resid, axis=1, keepdims=True))
    high = norms.astype(BF16).astype(F32)
    low = norms - high
    lane = lax.broadcasted_iota(jnp.int32, (8, LANES), 1)
    extra = jnp.zeros((8, LANES), F32)
    for part in range(width // 8):
        cut = slice(8 * part, 8 * part + 8)
        extra = jnp.where(lane == HIGH_LANE + part, high[cut], extra)
        extra = jnp.where(lane == LOW_LANE + part, low[cut], extra)
    update = math.sqrt(total_rows) * ortho
    below = jnp.zeros((LANES - padded, section_rows), F32)
    spare = lax.broadcasted_iota(jnp.int32, (16, 8, LANES), 2) >= width

    def turned(at):
        piece = update[:, at * section_rows : (at + 1) * section_rows]
        return jnp.concatenate([piece, below], axis=0).T.reshape(16, 8, LANES)

    def spill(rows, by):
        return jnp.where(spare, pltpu.roll(rows, by, 2), 0.0)

    for step, offset in enumerate(Y_OFFSETS):
        parts = []
        for first in (2 * step, 8 + 2 * step):
            one, two = turned(first), turned(first + 1)
            parts.append((jnp.where(b == 0, one, two), jnp.where(b == 0, two, one)))
        tiles = [jnp.where(core == 0, parts[0][i], parts[1][i]) for i in range(2)]
        tiles += [jnp.where(core == 0, parts[1][i], parts[0][i]) for i in range(2)]
        last = tiles[3]
        packed = jnp.concatenate(
            [
                tiles[0] + spill(last, 88),
                tiles[1] + spill(last, 48),
                tiles[2] + spill(last, 8) + extra,
            ],
            axis=1,
        )
        slots_ref[:, (y + offset) % 4] = packed.astype(BF16)


def products(sections, place, width, padded):
    columns = sections[0].shape[1]
    total_rows = sum(part.shape[0] for part in sections)
    return pl.pallas_call(
        lambda *refs: products_kernel(width, padded, *refs),
        in_specs=[pl.BlockSpec(memory_space=pltpu.SMEM)]
        + [pl.BlockSpec(memory_space=pl.ANY)] * len(sections),
        out_specs=pl.BlockSpec(memory_space=pltpu.VMEM),
        out_shape=jax.ShapeDtypeStruct((16, 4, SLOT_ROWS, LANES), BF16),
        scratch_shapes=[
            pltpu.VMEM((total_rows, columns), BF16),
            pltpu.SemaphoreType.DMA((len(sections),)),
        ],
        compiler_params=pltpu.CompilerParams(vmem_limit_bytes=VMEM_LIMIT),
        cost_estimate=pl.CostEstimate(
            flops=20 * padded * total_rows * columns,
            bytes_accessed=2 * total_rows * columns,
            transcendentals=0,
        ),
        name="products",
    )(place, *sections)


def regroup_kernel(width, place_ref, owner_ref, returned_ref, update_ref, norms_ref):
    y, z = place_ref[1], place_ref[3]
    matrices = update_ref.shape[0]
    lane = lax.broadcasted_iota(jnp.int32, (8, LANES), 1)
    for m in range(matrices):
        for at in range(16):
            core, source_y, b = at // 8, (at // 2) % 4, at % 2
            slot = returned_ref[core, m, b, source_y].astype(F32)
            last = jnp.where(
                lane < 40,
                pltpu.roll(slot[:8], 40, 1),
                jnp.where(lane < 80, pltpu.roll(slot[8:16], 80, 1), pltpu.roll(slot[16:], 120, 1)),
            )
            rows = jnp.concatenate([slot, last], axis=0).astype(BF16)
            update_ref[m, :, at * width : (at + 1) * width] = rows[:, :width]

        @pl.when(owner_ref[m] == y)
        def _():
            slot = returned_ref[z // 8, m, z % 2, (z // 2) % 4].astype(F32)
            turned = jnp.concatenate([slot[16:], slot], axis=0).T
            for part in range(width // 8):
                value = turned[HIGH_LANE + part : HIGH_LANE + part + 1, :8]
                value = value + turned[LOW_LANE + part : LOW_LANE + part + 1, :8]
                norms_ref[:, 8 * part : 8 * part + 8] = value


def regroup(returned, place, owner, width):
    matrices = returned.shape[1]
    smem = pl.BlockSpec(memory_space=pltpu.SMEM)
    vmem = pl.BlockSpec(memory_space=pltpu.VMEM)
    return pl.pallas_call(
        lambda *refs: regroup_kernel(width, *refs),
        in_specs=[smem, smem, vmem],
        out_specs=[vmem, vmem],
        out_shape=[
            jax.ShapeDtypeStruct((matrices, SLOT_ROWS + 8, 16 * width), BF16),
            jax.ShapeDtypeStruct((1, width), F32),
        ],
        compiler_params=pltpu.CompilerParams(vmem_limit_bytes=VMEM_LIMIT),
        name="regroup",
    )(place, owner, returned)


def on_device(grad, momentum, owner):
    matrices, rows, columns = grad.shape
    width = columns // 16
    padded = -(-width // 16) * 16
    core, y, z = lax.axis_index("core"), lax.axis_index("y"), lax.axis_index("z")
    place = jnp.stack([core, y, z % 2, z]).astype(jnp.int32)
    up = [(i, (i + 1) % 4) for i in range(4)]
    down = [((i + 1) % 4, i) for i in range(4)]
    swap = [(0, 1), (1, 0)]

    new_momentum, payload = momentum_step(grad, momentum)
    halves = lax.all_to_all(payload, "core", split_axis=0, concat_axis=0, tiled=True)
    mine = lax.all_to_all(
        halves.reshape(16, rows // 4, columns), "z", split_axis=0, concat_axis=0, tiled=True
    ).reshape(-1, columns)
    other = lax.ppermute(mine, "z", [(i, i ^ 1) for i in range(16)])
    mine_left = lax.ppermute(mine, "y", up)
    mine_right = lax.ppermute(mine, "y", down)
    other_left = lax.ppermute(other, "y", up)
    other_right = lax.ppermute(other, "y", down)
    mine_far = lax.ppermute(mine_left, "y", up)
    other_far = lax.ppermute(other_right, "y", down)
    here = jnp.concatenate([mine, other], axis=0)
    here, mine_left = lax.optimization_barrier((here, mine_left))
    here_swapped = lax.ppermute(here, "core", swap)
    near = jnp.concatenate([mine_left, other_left, mine_right, other_right], axis=0)
    near_swapped = lax.ppermute(near, "core", swap)
    far = jnp.concatenate([mine_far, other_far], axis=0)
    far_swapped = lax.ppermute(far, "core", swap)
    sections = [here, near, far, here_swapped, near_swapped, far_swapped]

    slots = products(sections, place, width, padded)
    returned = lax.all_to_all(
        slots.reshape(64, SLOT_ROWS, LANES), ("z", "y"), split_axis=0, concat_axis=0, tiled=True
    )
    returned = lax.all_to_all(
        returned.reshape(2, -1, SLOT_ROWS, LANES), "core", split_axis=0, concat_axis=0, tiled=True
    )
    returned = returned.reshape(2, matrices, 2, 4, SLOT_ROWS, LANES)
    out_update, norms = regroup(returned, place, owner.reshape(matrices), width)
    return new_momentum, out_update, norms


def solution(mesh):
    experts, shards = mesh.devices.shape
    split = Mesh(mesh.devices.reshape(experts // 2, 2, 4, shards // 4), ("x", "core", "y", "z"))
    groups, rows = ("x", "core"), ("y", "z")
    return jax.shard_map(
        on_device,
        mesh=split,
        in_specs=(P(groups, rows, None), P(groups, rows, None), P(groups, None)),
        out_specs=(P(groups, rows, None), P(groups, rows, None), P(groups, rows)),
        check_vma=False,
    )
```

```python
import math

import jax
import jax.numpy as jnp
from jax import lax
from jax.experimental import pallas as pl
from jax.experimental.pallas import tpu as pltpu
from jax.sharding import Mesh, PartitionSpec as P

DECAY = 0.95
COEF_A = 3.4445
COEF_B = -4.775
COEF_C = 2.0315
EPSILON = 1e-07

F32 = jnp.float32
BF16 = jnp.bfloat16
VMEM_LIMIT = 40 * 1024 * 1024
LANES = 128
Y_OFFSETS = (0, 3, 1, 2)
SECTION_SIZES = (4, 4, 4, 4)
SLOT_ROWS = 24
HIGH_LANE = 96
LOW_LANE = 112


def momentum_kernel(grad_ref, momentum_ref, new_ref, payload_ref):
    new = DECAY * momentum_ref[...] + grad_ref[...].astype(F32)
    new_ref[...] = new
    rounded = new.astype(BF16)
    half = payload_ref.shape[2]
    payload_ref[0] = rounded[:, :half]
    payload_ref[1] = rounded[:, half:]


def momentum_step(grad, momentum):
    matrices, rows, columns = grad.shape
    vmem = pl.BlockSpec(memory_space=pltpu.VMEM)
    return pl.pallas_call(
        momentum_kernel,
        in_specs=[vmem, vmem],
        out_specs=[vmem, vmem],
        out_shape=[
            jax.ShapeDtypeStruct(grad.shape, F32),
            jax.ShapeDtypeStruct((2, matrices, rows // 2, columns), BF16),
        ],
        compiler_params=pltpu.CompilerParams(vmem_limit_bytes=60 * 1024 * 1024),
        name="momentum_step",
    )(grad, momentum)


def times(block, x_ref):
    return jnp.dot(block, x_ref[...], preferred_element_type=F32)


def times_transposed(block, x_ref):
    return lax.dot_general(
        block, x_ref[...], (((1,), (1,)), ((), ())), preferred_element_type=F32
    )


def products_kernel(width, padded, place_ref, *refs):
    count = len(SECTION_SIZES)
    sections = refs[:count]
    slots_ref, x_ref, sems = refs[count:]
    core, y, b = place_ref[0], place_ref[1], place_ref[2]
    total_rows, columns = x_ref.shape
    section_rows = total_rows // 16
    copies = []
    at = 0
    for ref, size in zip(sections, SECTION_SIZES):
        rows = pl.ds(at * section_rows, size * section_rows)
        copies.append(pltpu.make_async_copy(ref, x_ref.at[rows], sems.at[len(copies)]))
        at += size
    for copy in copies:
        copy.start()
    total = jnp.zeros((16, columns), F32)
    at = 0
    for copy, size in zip(copies, SECTION_SIZES):
        copy.wait()
        for low in range(at * section_rows, (at + size) * section_rows, 16):
            piece = x_ref[low : low + 16, :].astype(F32)
            total = total + piece * piece
        at += size
    scale = 0.5 * math.sqrt(columns) / (jnp.sqrt(jnp.sum(total, keepdims=True)) + EPSILON)
    start = width * (core * 8 + y * 2 + b)
    row = lax.broadcasted_iota(jnp.int32, (padded, columns), 0)
    column = lax.broadcasted_iota(jnp.int32, (padded, columns), 1)
    identity = ((column == row + start) & (row < width)).astype(F32)
    own = times_transposed(identity.astype(BF16), x_ref).astype(BF16)
    gram = ((scale * scale) * times(own, x_ref)).astype(BF16)
    lifted = (scale * times_transposed(gram, x_ref)).astype(BF16)
    square = scale * times(lifted, x_ref)
    poly = (COEF_B * gram.astype(F32) + COEF_C * square).astype(BF16)
    ortho = scale * (COEF_A * own.astype(F32) + times_transposed(poly, x_ref))
    cross = (scale * times(ortho.astype(BF16), x_ref)).astype(BF16)
    first = (scale * times_transposed(cross, x_ref)).astype(BF16)
    second = (scale * times(first, x_ref)).astype(BF16)
    third = (scale * times_transposed(second, x_ref)).astype(BF16)
    fourth = scale * times(third, x_ref)
    resid = (
        COEF_A * cross.astype(F32) + COEF_B * second.astype(F32) + COEF_C * fourth - identity
    )
    norms = jnp.sqrt(jnp.sum(resid * resid, axis=1, keepdims=True))
    high = norms.astype(BF16).astype(F32)
    low = norms - high
    lane = lax.broadcasted_iota(jnp.int32, (8, LANES), 1)
    extra = jnp.zeros((8, LANES), F32)
    for part in range(width // 8):
        cut = slice(8 * part, 8 * part + 8)
        extra = jnp.where(lane == HIGH_LANE + part, high[cut], extra)
        extra = jnp.where(lane == LOW_LANE + part, low[cut], extra)
    update = math.sqrt(total_rows) * ortho
    below = jnp.zeros((LANES - padded, section_rows), F32)
    spare = lax.broadcasted_iota(jnp.int32, (16, 8, LANES), 2) >= width

    def turned(at):
        piece = update[:, at * section_rows : (at + 1) * section_rows]
        return jnp.concatenate([piece, below], axis=0).T.reshape(16, 8, LANES)

    def spill(rows, by):
        return jnp.where(spare, pltpu.roll(rows, by, 2), 0.0)

    for step, offset in enumerate(Y_OFFSETS):
        parts = []
        for first in (step, 8 + step):
            one, two = turned(first), turned(first + 4)
            parts.append((jnp.where(b == 0, one, two), jnp.where(b == 0, two, one)))
        tiles = [jnp.where(core == 0, parts[0][i], parts[1][i]) for i in range(2)]
        tiles += [jnp.where(core == 0, parts[1][i], parts[0][i]) for i in range(2)]
        last = tiles[3]
        packed = jnp.concatenate(
            [
                tiles[0] + spill(last, 88),
                tiles[1] + spill(last, 48),
                tiles[2] + spill(last, 8) + extra,
            ],
            axis=1,
        )
        slots_ref[:, (y + offset) % 4] = packed.astype(BF16)


def products(sections, place, width, padded):
    columns = sections[0].shape[1]
    total_rows = sum(part.shape[0] for part in sections)
    return pl.pallas_call(
        lambda *refs: products_kernel(width, padded, *refs),
        in_specs=[pl.BlockSpec(memory_space=pltpu.SMEM)]
        + [pl.BlockSpec(memory_space=pl.ANY)] * len(sections),
        out_specs=pl.BlockSpec(memory_space=pltpu.VMEM),
        out_shape=jax.ShapeDtypeStruct((16, 4, SLOT_ROWS, LANES), BF16),
        scratch_shapes=[
            pltpu.VMEM((total_rows, columns), BF16),
            pltpu.SemaphoreType.DMA((len(sections),)),
        ],
        compiler_params=pltpu.CompilerParams(vmem_limit_bytes=VMEM_LIMIT),
        cost_estimate=pl.CostEstimate(
            flops=20 * padded * total_rows * columns,
            bytes_accessed=2 * total_rows * columns,
            transcendentals=0,
        ),
        name="products",
    )(place, *sections)


def regroup_kernel(width, place_ref, owner_ref, returned_ref, update_ref, norms_ref):
    y, z = place_ref[1], place_ref[3]
    matrices = update_ref.shape[0]
    lane = lax.broadcasted_iota(jnp.int32, (8, LANES), 1)
    for m in range(matrices):
        for at in range(16):
            core, source_y, b = at // 8, (at // 2) % 4, at % 2
            slot = returned_ref[core, m, b, source_y].astype(F32)
            last = jnp.where(
                lane < 40,
                pltpu.roll(slot[:8], 40, 1),
                jnp.where(lane < 80, pltpu.roll(slot[8:16], 80, 1), pltpu.roll(slot[16:], 120, 1)),
            )
            rows = jnp.concatenate([slot, last], axis=0).astype(BF16)
            update_ref[m, :, at * width : (at + 1) * width] = rows[:, :width]

        @pl.when(owner_ref[m] == y)
        def _():
            slot = returned_ref[z // 8, m, z % 2, (z // 2) % 4].astype(F32)
            turned = jnp.concatenate([slot[16:], slot], axis=0).T
            for part in range(width // 8):
                value = turned[HIGH_LANE + part : HIGH_LANE + part + 1, :8]
                value = value + turned[LOW_LANE + part : LOW_LANE + part + 1, :8]
                norms_ref[:, 8 * part : 8 * part + 8] = value


def regroup(returned, place, owner, width):
    matrices = returned.shape[1]
    smem = pl.BlockSpec(memory_space=pltpu.SMEM)
    vmem = pl.BlockSpec(memory_space=pltpu.VMEM)
    return pl.pallas_call(
        lambda *refs: regroup_kernel(width, *refs),
        in_specs=[smem, smem, vmem],
        out_specs=[vmem, vmem],
        out_shape=[
            jax.ShapeDtypeStruct((matrices, SLOT_ROWS + 8, 16 * width), BF16),
            jax.ShapeDtypeStruct((1, width), F32),
        ],
        compiler_params=pltpu.CompilerParams(vmem_limit_bytes=VMEM_LIMIT),
        name="regroup",
    )(place, owner, returned)


def on_device(grad, momentum, owner):
    matrices, rows, columns = grad.shape
    width = columns // 16
    padded = -(-width // 16) * 16
    core, y, z = lax.axis_index("core"), lax.axis_index("y"), lax.axis_index("z")
    place = jnp.stack([core, y, z % 2, z]).astype(jnp.int32)
    up = [(i, (i + 1) % 4) for i in range(4)]
    down = [((i + 1) % 4, i) for i in range(4)]
    swap = [(0, 1), (1, 0)]

    new_momentum, payload = momentum_step(grad, momentum)
    halves = lax.all_to_all(payload, "core", split_axis=0, concat_axis=0, tiled=True)
    mine = lax.all_to_all(
        halves.reshape(16, rows // 4, columns), "z", split_axis=0, concat_axis=0, tiled=True
    ).reshape(-1, columns)
    other = lax.ppermute(mine, "z", [(i, i ^ 1) for i in range(16)])
    mine_left = lax.ppermute(mine, "y", up)
    mine_right = lax.ppermute(mine, "y", down)
    other_left = lax.ppermute(other, "y", up)
    other_right = lax.ppermute(other, "y", down)
    mine_far = lax.ppermute(mine_left, "y", up)
    other_far = lax.ppermute(other_right, "y", down)
    mine = jnp.concatenate([mine, mine_left, mine_right, mine_far], axis=0)
    mine_swapped = lax.ppermute(mine, "core", swap)
    other = jnp.concatenate([other, other_left, other_right, other_far], axis=0)
    other_swapped = lax.ppermute(other, "core", swap)
    sections = [mine, other, mine_swapped, other_swapped]

    slots = products(sections, place, width, padded)
    returned = lax.all_to_all(
        slots.reshape(64, SLOT_ROWS, LANES), ("z", "y"), split_axis=0, concat_axis=0, tiled=True
    )
    returned = lax.all_to_all(
        returned.reshape(2, -1, SLOT_ROWS, LANES), "core", split_axis=0, concat_axis=0, tiled=True
    )
    returned = returned.reshape(2, matrices, 2, 4, SLOT_ROWS, LANES)
    out_update, norms = regroup(returned, place, owner.reshape(matrices), width)
    return new_momentum, out_update, norms


def solution(mesh):
    experts, shards = mesh.devices.shape
    split = Mesh(mesh.devices.reshape(experts // 2, 2, 4, shards // 4), ("x", "core", "y", "z"))
    groups, rows = ("x", "core"), ("y", "z")
    return jax.shard_map(
        on_device,
        mesh=split,
        in_specs=(P(groups, rows, None), P(groups, rows, None), P(groups, None)),
        out_specs=(P(groups, rows, None), P(groups, rows, None), P(groups, rows)),
        check_vma=False,
    )
```

```python
import math

import jax
import jax.numpy as jnp
from jax import lax
from jax.experimental import pallas as pl
from jax.experimental.pallas import tpu as pltpu
from jax.sharding import Mesh, PartitionSpec as P

DECAY = 0.95
COEF_A = 3.4445
COEF_B = -4.775
COEF_C = 2.0315
EPSILON = 1e-07

F32 = jnp.float32
BF16 = jnp.bfloat16
VMEM_LIMIT = 36 * 1024 * 1024
LANES = 128
Y_OFFSETS = (0, 3, 1, 2)
STRIP = 256
SLOT_ROWS = 24
HIGH_LANE = 96
LOW_LANE = 112


def momentum_kernel(place_ref, grad_ref, momentum_ref, new_ref, keep_ref, send_ref):
    new = DECAY * momentum_ref[...] + grad_ref[...].astype(F32)
    new_ref[...] = new
    half = keep_ref.shape[1]
    first = place_ref[0] == 0
    keep_ref[...] = jnp.where(first, new[:, :half], new[:, half:]).astype(BF16)
    send_ref[...] = jnp.where(first, new[:, half:], new[:, :half]).astype(BF16)


def momentum_step(place, grad, momentum):
    matrices, rows, columns = grad.shape
    vmem = pl.BlockSpec(memory_space=pltpu.VMEM)
    half = jax.ShapeDtypeStruct((matrices, rows // 2, columns), BF16)
    return pl.pallas_call(
        momentum_kernel,
        in_specs=[pl.BlockSpec(memory_space=pltpu.SMEM), vmem, vmem],
        out_specs=[vmem, vmem, vmem],
        out_shape=[jax.ShapeDtypeStruct(grad.shape, F32), half, half],
        compiler_params=pltpu.CompilerParams(vmem_limit_bytes=60 * 1024 * 1024),
        name="momentum_step",
    )(place, grad, momentum)


def strips(columns):
    return [(at, min(STRIP, columns - at)) for at in range(0, columns, STRIP)]


def gram_strip(x_ref, at, size):
    return lax.dot_general(
        x_ref[:, at : at + size],
        x_ref[:, at:],
        (((0,), (0,)), ((), ())),
        preferred_element_type=F32,
    )


def gram_part_kernel(one_ref, two_ref, part_ref):
    for at, size in strips(one_ref.shape[1]):
        total = gram_strip(one_ref, at, size) + gram_strip(two_ref, at, size)
        part_ref[at : at + size, at:] = total


def gram_part(one, two):
    rows, columns = one.shape
    vmem = pl.BlockSpec(memory_space=pltpu.VMEM)
    return pl.pallas_call(
        gram_part_kernel,
        in_specs=[vmem, vmem],
        out_specs=vmem,
        out_shape=jax.ShapeDtypeStruct((columns, columns), F32),
        compiler_params=pltpu.CompilerParams(vmem_limit_bytes=24 * 1024 * 1024),
        cost_estimate=pl.CostEstimate(
            flops=2 * rows * columns * columns, bytes_accessed=0, transcendentals=0
        ),
        name="gram_part",
    )(one, two)


def times(block, matrix_ref):
    return jnp.dot(block, matrix_ref[...], preferred_element_type=F32)


def times_transposed(block, x_ref):
    return lax.dot_general(
        block, x_ref[...], (((1,), (1,)), ((), ())), preferred_element_type=F32
    )


def products_kernel(
    width, padded, place_ref, mine_ref, other_ref, mine2_ref, other2_ref, part_ref,
    slots_ref, gram_ref,
):
    sections = (mine_ref, other_ref, mine2_ref, other2_ref)
    core, y, b = place_ref[0], place_ref[1], place_ref[2]
    columns = mine_ref.shape[1]
    total_rows = 4 * mine_ref.shape[0]
    section_rows = total_rows // 16
    cuts = strips(columns)
    squares = jnp.zeros((1, 1), F32)
    for index, (at, size) in enumerate(cuts):
        piece = part_ref[at : at + size, at:]
        piece = piece + gram_strip(other_ref, at, size) + gram_strip(other2_ref, at, size)
        row = lax.broadcasted_iota(jnp.int32, (size, size), 0)
        column = lax.broadcasted_iota(jnp.int32, (size, size), 1)
        diagonal = jnp.where(row == column, piece[:, :size], 0.0)
        squares = squares + jnp.sum(diagonal, keepdims=True)
        gram_ref[at : at + size, at:] = piece.astype(BF16)
        for low, count in cuts[index + 1 :]:
            gram_ref[low : low + count, at : at + size] = gram_ref[
                at : at + size, low : low + count
            ].T
    scale = 0.5 * math.sqrt(columns) / (jnp.sqrt(squares) + EPSILON)
    scale_squared = scale * scale
    start = width * (core * 8 + y * 2 + b)
    row = lax.broadcasted_iota(jnp.int32, (padded, columns), 0)
    column = lax.broadcasted_iota(jnp.int32, (padded, columns), 1)
    identity = ((column == row + start) & (row < width)).astype(F32)
    aligned = start // 16 * 16
    found = gram_ref[pl.ds(pl.multiple_of(aligned, 16), padded), :].astype(F32)
    moved = jnp.concatenate([found[8:], jnp.zeros((8, columns), F32)], axis=0)
    found = jnp.where(row < width, jnp.where(start == aligned, found, moved), 0.0)
    gram = (scale_squared * found).astype(BF16)
    square = scale_squared * times(gram, gram_ref)
    poly = COEF_B * gram.astype(F32) + COEF_C * square
    mixed = (COEF_A * identity + poly).astype(BF16)
    poly = poly.astype(BF16)
    cross = COEF_A * gram.astype(F32) + scale_squared * times(poly, gram_ref)
    cross = cross.astype(BF16)
    second = (scale_squared * times(cross, gram_ref)).astype(BF16)
    fourth = scale_squared * times(second, gram_ref)
    resid = (
        COEF_A * cross.astype(F32) + COEF_B * second.astype(F32) + COEF_C * fourth - identity
    )
    norms = jnp.sqrt(jnp.sum(resid * resid, axis=1, keepdims=True))
    high = norms.astype(BF16).astype(F32)
    low = norms - high
    lane = lax.broadcasted_iota(jnp.int32, (8, LANES), 1)
    extra = jnp.zeros((8, LANES), F32)
    for part in range(width // 8):
        cut = slice(8 * part, 8 * part + 8)
        extra = jnp.where(lane == HIGH_LANE + part, high[cut], extra)
        extra = jnp.where(lane == LOW_LANE + part, low[cut], extra)
    factor = math.sqrt(total_rows) * scale
    updates = [factor * times_transposed(mixed, ref) for ref in sections]
    below = jnp.zeros((LANES - padded, section_rows), F32)
    spare = lax.broadcasted_iota(jnp.int32, (16, 8, LANES), 2) >= width

    def turned(at):
        low = at % 4 * section_rows
        piece = updates[at // 4][:, low : low + section_rows]
        return jnp.concatenate([piece, below], axis=0).T.reshape(16, 8, LANES)

    def spill(rows, by):
        return jnp.where(spare, pltpu.roll(rows, by, 2), 0.0)

    for step, offset in enumerate(Y_OFFSETS):
        parts = []
        for first in (step, 8 + step):
            one, two = turned(first), turned(first + 4)
            parts.append((jnp.where(b == 0, one, two), jnp.where(b == 0, two, one)))
        tiles = [jnp.where(core == 0, parts[0][i], parts[1][i]) for i in range(2)]
        tiles += [jnp.where(core == 0, parts[1][i], parts[0][i]) for i in range(2)]
        last = tiles[3]
        packed = jnp.concatenate(
            [
                tiles[0] + spill(last, 88),
                tiles[1] + spill(last, 48),
                tiles[2] + spill(last, 8) + extra,
            ],
            axis=1,
        )
        slots_ref[:, (y + offset) % 4] = packed.astype(BF16)


def products(sections, part, place, width, padded):
    rows, columns = sections[0].shape
    vmem = pl.BlockSpec(memory_space=pltpu.VMEM)
    return pl.pallas_call(
        lambda *refs: products_kernel(width, padded, *refs),
        in_specs=[pl.BlockSpec(memory_space=pltpu.SMEM)] + [vmem] * 5,
        out_specs=vmem,
        out_shape=jax.ShapeDtypeStruct((16, 4, SLOT_ROWS, LANES), BF16),
        scratch_shapes=[pltpu.VMEM((columns, columns), BF16)],
        compiler_params=pltpu.CompilerParams(vmem_limit_bytes=VMEM_LIMIT),
        cost_estimate=pl.CostEstimate(
            flops=8 * rows * columns * columns, bytes_accessed=0, transcendentals=0
        ),
        name="products",
    )(place, *sections, part)


def regroup_kernel(width, place_ref, owner_ref, returned_ref, update_ref, norms_ref):
    y, z = place_ref[1], place_ref[3]
    matrices = update_ref.shape[0]
    lane = lax.broadcasted_iota(jnp.int32, (8, LANES), 1)
    for m in range(matrices):
        for at in range(16):
            core, source_y, b = at // 8, (at // 2) % 4, at % 2
            slot = returned_ref[core, m, b, source_y].astype(F32)
            last = jnp.where(
                lane < 40,
                pltpu.roll(slot[:8], 40, 1),
                jnp.where(lane < 80, pltpu.roll(slot[8:16], 80, 1), pltpu.roll(slot[16:], 120, 1)),
            )
            rows = jnp.concatenate([slot, last], axis=0).astype(BF16)
            update_ref[m, :, at * width : (at + 1) * width] = rows[:, :width]

        @pl.when(owner_ref[m] == y)
        def _():
            slot = returned_ref[z // 8, m, z % 2, (z // 2) % 4].astype(F32)
            turned = jnp.concatenate([slot[16:], slot], axis=0).T
            for part in range(width // 8):
                value = turned[HIGH_LANE + part : HIGH_LANE + part + 1, :8]
                value = value + turned[LOW_LANE + part : LOW_LANE + part + 1, :8]
                norms_ref[:, 8 * part : 8 * part + 8] = value


def regroup(returned, place, owner, width):
    matrices = returned.shape[1]
    smem = pl.BlockSpec(memory_space=pltpu.SMEM)
    vmem = pl.BlockSpec(memory_space=pltpu.VMEM)
    return pl.pallas_call(
        lambda *refs: regroup_kernel(width, *refs),
        in_specs=[smem, smem, vmem],
        out_specs=[vmem, vmem],
        out_shape=[
            jax.ShapeDtypeStruct((matrices, SLOT_ROWS + 8, 16 * width), BF16),
            jax.ShapeDtypeStruct((1, width), F32),
        ],
        compiler_params=pltpu.CompilerParams(vmem_limit_bytes=VMEM_LIMIT),
        name="regroup",
    )(place, owner, returned)


def on_device(grad, momentum, owner):
    matrices, rows, columns = grad.shape
    width = columns // 16
    padded = -(-width // 16) * 16
    core, y, z = lax.axis_index("core"), lax.axis_index("y"), lax.axis_index("z")
    place = jnp.stack([core, y, z % 2, z]).astype(jnp.int32)
    up = [(i, (i + 1) % 4) for i in range(4)]
    down = [((i + 1) % 4, i) for i in range(4)]
    swap = [(0, 1), (1, 0)]

    new_momentum, keep, send = momentum_step(place, grad, momentum)
    got = lax.ppermute(send, "core", swap)
    halves = jnp.where(
        core == 0, jnp.concatenate([keep, got], axis=0), jnp.concatenate([got, keep], axis=0)
    )
    mine = lax.all_to_all(
        halves.reshape(16, rows // 4, columns), "z", split_axis=0, concat_axis=0, tiled=True
    ).reshape(-1, columns)
    other = lax.ppermute(mine, "z", [(i, i ^ 1) for i in range(16)])
    mine_left = lax.ppermute(mine, "y", up)
    mine_right = lax.ppermute(mine, "y", down)
    other_left = lax.ppermute(other, "y", up)
    other_right = lax.ppermute(other, "y", down)
    mine_far = lax.ppermute(mine_left, "y", up)
    other_far = lax.ppermute(other_right, "y", down)
    mine = jnp.concatenate([mine, mine_left, mine_right, mine_far], axis=0)
    mine_swapped = lax.ppermute(mine, "core", swap)
    other = jnp.concatenate([other, other_left, other_right, other_far], axis=0)
    other_swapped = lax.ppermute(other, "core", swap)
    part = gram_part(mine, mine_swapped)
    slots = products([mine, other, mine_swapped, other_swapped], part, place, width, padded)
    returned = lax.all_to_all(
        slots.reshape(64, SLOT_ROWS, LANES), ("z", "y"), split_axis=0, concat_axis=0, tiled=True
    )
    returned = lax.all_to_all(
        returned.reshape(2, -1, SLOT_ROWS, LANES), "core", split_axis=0, concat_axis=0, tiled=True
    )
    returned = returned.reshape(2, matrices, 2, 4, SLOT_ROWS, LANES)
    out_update, norms = regroup(returned, place, owner.reshape(matrices), width)
    return new_momentum, out_update, norms


def solution(mesh):
    experts, shards = mesh.devices.shape
    split = Mesh(mesh.devices.reshape(experts // 2, 2, 4, shards // 4), ("x", "core", "y", "z"))
    groups, rows = ("x", "core"), ("y", "z")
    return jax.shard_map(
        on_device,
        mesh=split,
        in_specs=(P(groups, rows, None), P(groups, rows, None), P(groups, None)),
        out_specs=(P(groups, rows, None), P(groups, rows, None), P(groups, rows)),
        check_vma=False,
    )
```

```python
import math

import jax
import jax.numpy as jnp
from jax import lax
from jax.experimental import pallas as pl
from jax.experimental.pallas import tpu as pltpu
from jax.sharding import Mesh, PartitionSpec as P

DECAY = 0.95
COEF_A = 3.4445
COEF_B = -4.775
COEF_C = 2.0315
EPSILON = 1e-07

F32 = jnp.float32
BF16 = jnp.bfloat16
VMEM_LIMIT = 36 * 1024 * 1024
LANES = 128
STRIP = 256
LOW_LANE = 64


def momentum_kernel(grad_ref, momentum_ref, new_ref, keep_ref, send_ref):
    core = lax.axis_index("core")
    new = DECAY * momentum_ref[...] + grad_ref[...].astype(F32)
    new_ref[...] = new
    half = send_ref.shape[1]
    first = core == 0
    keep_ref[core] = jnp.where(first, new[:, :half], new[:, half:]).astype(BF16)
    send_ref[...] = jnp.where(first, new[:, half:], new[:, :half]).astype(BF16)


def momentum_step(grad, momentum):
    matrices, rows, columns = grad.shape
    vmem = pl.BlockSpec(memory_space=pltpu.VMEM)
    half = (matrices, rows // 2, columns)
    return pl.pallas_call(
        momentum_kernel,
        in_specs=[vmem, vmem],
        out_specs=[vmem, vmem, vmem],
        out_shape=[
            jax.ShapeDtypeStruct(grad.shape, F32),
            jax.ShapeDtypeStruct((2,) + half, BF16),
            jax.ShapeDtypeStruct(half, BF16),
        ],
        compiler_params=pltpu.CompilerParams(vmem_limit_bytes=60 * 1024 * 1024),
        name="momentum_step",
    )(grad, momentum)


def strips(columns):
    return [(at, min(STRIP, columns - at)) for at in range(0, columns, STRIP)]


def gram_strip(x_ref, at, size):
    return lax.dot_general(
        x_ref[:, at : at + size],
        x_ref[:, at:],
        (((0,), (0,)), ((), ())),
        preferred_element_type=F32,
    )


def gram_part_kernel(one_ref, two_ref, part_ref):
    for at, size in strips(one_ref.shape[1]):
        total = gram_strip(one_ref, at, size) + gram_strip(two_ref, at, size)
        part_ref[at : at + size, at:] = total


def gram_part(one, two):
    rows, columns = one.shape
    vmem = pl.BlockSpec(memory_space=pltpu.VMEM)
    return pl.pallas_call(
        gram_part_kernel,
        in_specs=[vmem, vmem],
        out_specs=vmem,
        out_shape=jax.ShapeDtypeStruct((columns, columns), F32),
        compiler_params=pltpu.CompilerParams(vmem_limit_bytes=24 * 1024 * 1024),
        cost_estimate=pl.CostEstimate(
            flops=2 * rows * columns * columns, bytes_accessed=0, transcendentals=0
        ),
        name="gram_part",
    )(one, two)


def times(block, matrix):
    return jnp.dot(block, matrix, preferred_element_type=F32)


def mirror(matrix_ref, cuts, index):
    at, size = cuts[index]
    for low, count in cuts[index + 1 :]:
        matrix_ref[low : low + count, at : at + size] = matrix_ref[
            at : at + size, low : low + count
        ].T


def products_kernel(
    mine_ref, other_ref, mine2_ref, other2_ref, part_ref, slots_ref, gram_ref, poly_ref
):
    core, b = lax.axis_index("core"), lax.axis_index("z") % 2
    section_rows, columns = mine_ref.shape
    total_rows = 4 * section_rows
    cuts = strips(columns)
    squares = jnp.zeros((1, 1), F32)
    for index, (at, size) in enumerate(cuts):
        piece = part_ref[at : at + size, at:]
        piece = piece + gram_strip(other_ref, at, size) + gram_strip(other2_ref, at, size)
        row = lax.broadcasted_iota(jnp.int32, (size, size), 0)
        column = lax.broadcasted_iota(jnp.int32, (size, size), 1)
        diagonal = jnp.where(row == column, piece[:, :size], 0.0)
        squares = squares + jnp.sum(diagonal, keepdims=True)
        gram_ref[at : at + size, at:] = piece.astype(BF16)
        mirror(gram_ref, cuts, index)
    scale = 0.5 * math.sqrt(columns) / (jnp.sqrt(squares) + EPSILON)
    scale_squared = scale * scale
    for index, (at, size) in enumerate(cuts):
        rows = gram_ref[at : at + size, :]
        square = scale_squared * times(rows, gram_ref[:, at:])
        poly = scale_squared * (COEF_B * rows[:, at:].astype(F32) + COEF_C * square)
        poly_ref[at : at + size, at:] = poly.astype(BF16)
        mirror(poly_ref, cuts, index)
    own = mine_ref[: total_rows // 16, :]
    ortho = COEF_A * own.astype(F32) + times(own, poly_ref[...])
    update = (math.sqrt(total_rows) * scale) * ortho
    slots_ref[:, :, :columns] = update.reshape(16, -1, columns).astype(BF16)

    width = columns // 4
    start = pl.multiple_of(width * (core * 2 + b), 16)
    block = pl.ds(start, width)
    row = lax.broadcasted_iota(jnp.int32, (width, columns), 0)
    column = lax.broadcasted_iota(jnp.int32, (width, columns), 1)
    cross = COEF_A * gram_ref[block, :].astype(F32) + times(poly_ref[block, :], gram_ref[...])
    cross = (scale_squared * cross).astype(BF16)
    resid = COEF_A * cross.astype(F32) + times(cross, poly_ref[...])
    resid = resid - (column == row + start).astype(F32)
    norms = jnp.sqrt(jnp.sum(resid * resid, axis=1, keepdims=True))
    high = norms.astype(BF16).astype(F32)
    low = norms - high
    lane = lax.broadcasted_iota(jnp.int32, (8, LANES), 1)
    extra = jnp.zeros((8, LANES), F32)
    for part in range(width // 8):
        cut = slice(8 * part, 8 * part + 8)
        extra = jnp.where(lane == part, high[cut], extra)
        extra = jnp.where(lane == LOW_LANE + part, low[cut], extra)
    slots_ref[:, :, columns:] = jnp.broadcast_to(extra[None], (16, 8, LANES)).astype(BF16)


def products(sections, part):
    rows, columns = sections[0].shape
    vmem = pl.BlockSpec(memory_space=pltpu.VMEM)
    return pl.pallas_call(
        products_kernel,
        in_specs=[vmem] * 5,
        out_specs=vmem,
        out_shape=jax.ShapeDtypeStruct((16, 8, columns + LANES), BF16),
        scratch_shapes=[pltpu.VMEM((columns, columns), BF16)] * 2,
        compiler_params=pltpu.CompilerParams(vmem_limit_bytes=VMEM_LIMIT),
        cost_estimate=pl.CostEstimate(
            flops=12 * rows * columns * columns, bytes_accessed=0, transcendentals=0
        ),
        name="products",
    )(*sections, part)


def regroup_kernel(owner_ref, near_ref, far_ref, update_ref, norms_ref):
    core, y, z = lax.axis_index("core"), lax.axis_index("y"), lax.axis_index("z")
    matrices, rows, columns = update_ref.shape
    half = rows // 2
    near, far = near_ref[core], far_ref[core]
    update_ref[:, :half] = jnp.where(core == 0, near, far)[:, :, :columns]
    update_ref[:, half:] = jnp.where(core == 0, far, near)[:, :, :columns]
    near, far = near[:, :, columns:].astype(F32), far[:, :, columns:].astype(F32)
    tiles = jnp.where(z // 8 == core, near, far)
    tiles = jnp.where(z // 4 % 2 == 0, tiles[:, :8], tiles[:, 8:])
    tile = tiles[0]
    for m in range(1, matrices):
        tile = jnp.where(owner_ref[m] == y, tiles[m], tile)
    turned = jnp.concatenate([tile] * 4, axis=0).T
    count = norms_ref.shape[1] // 8
    for quarter in range(4):

        @pl.when(z % 4 == quarter)
        def _():
            for part in range(count):
                at = quarter * count + part
                value = turned[at : at + 1, :8] + turned[LOW_LANE + at : LOW_LANE + at + 1, :8]
                norms_ref[:, 8 * part : 8 * part + 8] = value


def regroup(owner, near, far):
    matrices, half = near.shape[1:3]
    columns = near.shape[3] - LANES
    vmem = pl.BlockSpec(memory_space=pltpu.VMEM)
    return pl.pallas_call(
        regroup_kernel,
        in_specs=[pl.BlockSpec(memory_space=pltpu.SMEM), vmem, vmem],
        out_specs=[vmem, vmem],
        out_shape=[
            jax.ShapeDtypeStruct((matrices, 2 * half, columns), BF16),
            jax.ShapeDtypeStruct((1, columns // 16), F32),
        ],
        compiler_params=pltpu.CompilerParams(vmem_limit_bytes=VMEM_LIMIT),
        name="regroup",
    )(owner, near, far)


def on_device(grad, momentum, owner):
    matrices, rows, columns = grad.shape
    core = lax.axis_index("core")
    up = [(i, (i + 1) % 4) for i in range(4)]
    down = [((i + 1) % 4, i) for i in range(4)]
    swap = [(0, 1), (1, 0)]

    new_momentum, halves, send = momentum_step(grad, momentum)
    got = lax.ppermute(send, "core", swap)
    halves = lax.dynamic_update_slice_in_dim(halves, got[None], 1 - core, 0)
    mine = lax.all_to_all(
        halves.reshape(16, rows // 4, columns), "z", split_axis=0, concat_axis=0, tiled=True
    ).reshape(-1, columns)
    other = lax.ppermute(mine, "z", [(i, i ^ 1) for i in range(16)])
    mine_left = lax.ppermute(mine, "y", up)
    mine_right = lax.ppermute(mine, "y", down)
    other_left = lax.ppermute(other, "y", up)
    other_right = lax.ppermute(other, "y", down)
    mine_far = lax.ppermute(mine_left, "y", up)
    other_far = lax.ppermute(other_right, "y", down)
    mine = jnp.concatenate([mine, mine_left, mine_right, mine_far], axis=0)
    mine_swapped = lax.ppermute(mine, "core", swap)
    other = jnp.concatenate([other, other_left, other_right, other_far], axis=0)
    other_swapped = lax.ppermute(other, "core", swap)
    part = gram_part(mine, mine_swapped)
    slots = products([mine, other, mine_swapped, other_swapped], part)
    near = lax.all_to_all(slots, "z", split_axis=0, concat_axis=0, tiled=True)
    near = near.reshape(2, matrices, rows // 2, columns + LANES)
    far = lax.ppermute(near, "core", swap)
    out_update, norms = regroup(owner.reshape(matrices), near, far)
    return new_momentum, out_update, norms


def solution(mesh):
    experts, shards = mesh.devices.shape
    split = Mesh(mesh.devices.reshape(experts // 2, 2, 4, shards // 4), ("x", "core", "y", "z"))
    groups, rows = ("x", "core"), ("y", "z")
    return jax.shard_map(
        on_device,
        mesh=split,
        in_specs=(P(groups, rows, None), P(groups, rows, None), P(groups, None)),
        out_specs=(P(groups, rows, None), P(groups, rows, None), P(groups, rows)),
        check_vma=False,
    )
```

```python
import math

import jax
import jax.numpy as jnp
from jax import lax
from jax.experimental import pallas as pl
from jax.experimental.pallas import tpu as pltpu
from jax.sharding import Mesh, PartitionSpec as P

DECAY = 0.95
COEF_A = 3.4445
COEF_B = -4.775
COEF_C = 2.0315
EPSILON = 1e-07

F32 = jnp.float32
BF16 = jnp.bfloat16
VMEM_LIMIT = 36 * 1024 * 1024
LANES = 128
STRIP = 256
LOW_LANE = 64


def momentum_kernel(grad_ref, momentum_ref, new_ref, keep_ref, send_ref):
    core = lax.axis_index("core")
    new = DECAY * momentum_ref[...] + grad_ref[...].astype(F32)
    new_ref[...] = new
    half = send_ref.shape[1]
    first = core == 0
    keep_ref[core] = jnp.where(first, new[:, :half], new[:, half:]).astype(BF16)
    send_ref[...] = jnp.where(first, new[:, half:], new[:, :half]).astype(BF16)


def momentum_step(grad, momentum):
    matrices, rows, columns = grad.shape
    vmem = pl.BlockSpec(memory_space=pltpu.VMEM)
    half = (matrices, rows // 2, columns)
    return pl.pallas_call(
        momentum_kernel,
        in_specs=[vmem, vmem],
        out_specs=[vmem, vmem, vmem],
        out_shape=[
            jax.ShapeDtypeStruct(grad.shape, F32),
            jax.ShapeDtypeStruct((2,) + half, BF16),
            jax.ShapeDtypeStruct(half, BF16),
        ],
        compiler_params=pltpu.CompilerParams(vmem_limit_bytes=60 * 1024 * 1024),
        name="momentum_step",
    )(grad, momentum)


def strips(columns):
    return [(at, min(STRIP, columns - at)) for at in range(0, columns, STRIP)]


def gram_strip(x_ref, at, size):
    return lax.dot_general(
        x_ref[:, at : at + size],
        x_ref[:, at:],
        (((0,), (0,)), ((), ())),
        preferred_element_type=F32,
    )


def gram_sum(refs, at, size):
    total = gram_strip(refs[0], at, size)
    for ref in refs[1:]:
        total = total + gram_strip(ref, at, size)
    return total


def gram_part_kernel(*refs):
    part_ref = refs[-1]
    for at, size in strips(part_ref.shape[1]):
        part_ref[at : at + size, at:] = gram_sum(refs[:-1], at, size)


def gram_part(*blocks):
    rows, columns = sum(block.shape[0] for block in blocks), blocks[0].shape[1]
    vmem = pl.BlockSpec(memory_space=pltpu.VMEM)
    return pl.pallas_call(
        gram_part_kernel,
        in_specs=[vmem] * len(blocks),
        out_specs=vmem,
        out_shape=jax.ShapeDtypeStruct((columns, columns), F32),
        compiler_params=pltpu.CompilerParams(vmem_limit_bytes=24 * 1024 * 1024),
        cost_estimate=pl.CostEstimate(
            flops=2 * rows * columns * columns, bytes_accessed=0, transcendentals=0
        ),
        name="gram_part",
    )(*blocks)


def times(block, matrix):
    return jnp.dot(block, matrix, preferred_element_type=F32)


def mirror(matrix_ref, cuts, index):
    at, size = cuts[index]
    for low, count in cuts[index + 1 :]:
        matrix_ref[low : low + count, at : at + size] = matrix_ref[
            at : at + size, low : low + count
        ].T


def products_kernel(mine_ref, part_ref, *refs):
    slots_ref, gram_ref, poly_ref = refs[-3:]
    core, b = lax.axis_index("core"), lax.axis_index("z") % 2
    columns = mine_ref.shape[1]
    own_rows = slots_ref.shape[0] * slots_ref.shape[1]
    total_rows = 16 * own_rows
    cuts = strips(columns)
    squares = jnp.zeros((1, 1), F32)
    for index, (at, size) in enumerate(cuts):
        piece = part_ref[at : at + size, at:] + gram_sum(refs[:-3], at, size)
        row = lax.broadcasted_iota(jnp.int32, (size, size), 0)
        column = lax.broadcasted_iota(jnp.int32, (size, size), 1)
        diagonal = jnp.where(row == column, piece[:, :size], 0.0)
        squares = squares + jnp.sum(diagonal, keepdims=True)
        gram_ref[at : at + size, at:] = piece.astype(BF16)
        mirror(gram_ref, cuts, index)
    scale = 0.5 * math.sqrt(columns) / (jnp.sqrt(squares) + EPSILON)
    scale_squared = scale * scale
    for index, (at, size) in enumerate(cuts):
        rows = gram_ref[at : at + size, :]
        square = scale_squared * times(rows, gram_ref[:, at:])
        poly = scale_squared * (COEF_B * rows[:, at:].astype(F32) + COEF_C * square)
        poly_ref[at : at + size, at:] = poly.astype(BF16)
        mirror(poly_ref, cuts, index)
    own = mine_ref[:own_rows, :]
    ortho = COEF_A * own.astype(F32) + times(own, poly_ref[...])
    update = (math.sqrt(total_rows) * scale) * ortho
    slots_ref[:, :, :columns] = update.reshape(16, -1, columns).astype(BF16)

    width = columns // 4
    start = pl.multiple_of(width * (core * 2 + b), 16)
    block = pl.ds(start, width)
    row = lax.broadcasted_iota(jnp.int32, (width, columns), 0)
    column = lax.broadcasted_iota(jnp.int32, (width, columns), 1)
    cross = COEF_A * gram_ref[block, :].astype(F32) + times(poly_ref[block, :], gram_ref[...])
    cross = (scale_squared * cross).astype(BF16)
    resid = COEF_A * cross.astype(F32) + times(cross, poly_ref[...])
    resid = resid - (column == row + start).astype(F32)
    norms = jnp.sqrt(jnp.sum(resid * resid, axis=1, keepdims=True))
    high = norms.astype(BF16).astype(F32)
    low = norms - high
    lane = lax.broadcasted_iota(jnp.int32, (8, LANES), 1)
    extra = jnp.zeros((8, LANES), F32)
    for part in range(width // 8):
        cut = slice(8 * part, 8 * part + 8)
        extra = jnp.where(lane == part, high[cut], extra)
        extra = jnp.where(lane == LOW_LANE + part, low[cut], extra)
    slots_ref[:, :, columns:] = jnp.broadcast_to(extra[None], (16, 8, LANES)).astype(BF16)


def products(mine, part, *blocks):
    columns = mine.shape[1]
    vmem = pl.BlockSpec(memory_space=pltpu.VMEM)
    return pl.pallas_call(
        products_kernel,
        in_specs=[vmem] * (2 + len(blocks)),
        out_specs=vmem,
        out_shape=jax.ShapeDtypeStruct((16, 8, columns + LANES), BF16),
        scratch_shapes=[pltpu.VMEM((columns, columns), BF16)] * 2,
        compiler_params=pltpu.CompilerParams(vmem_limit_bytes=VMEM_LIMIT),
        cost_estimate=pl.CostEstimate(
            flops=12 * 512 * columns * columns, bytes_accessed=0, transcendentals=0
        ),
        name="products",
    )(mine, part, *blocks)


def regroup_kernel(owner_ref, near_ref, far_ref, update_ref, norms_ref):
    core, y, z = lax.axis_index("core"), lax.axis_index("y"), lax.axis_index("z")
    matrices, rows, columns = update_ref.shape
    half = rows // 2
    near, far = near_ref[core], far_ref[core]
    update_ref[:, :half] = jnp.where(core == 0, near, far)[:, :, :columns]
    update_ref[:, half:] = jnp.where(core == 0, far, near)[:, :, :columns]
    near, far = near[:, :, columns:].astype(F32), far[:, :, columns:].astype(F32)
    tiles = jnp.where(z // 8 == core, near, far)
    tiles = jnp.where(z // 4 % 2 == 0, tiles[:, :8], tiles[:, 8:])
    tile = tiles[0]
    for m in range(1, matrices):
        tile = jnp.where(owner_ref[m] == y, tiles[m], tile)
    turned = jnp.concatenate([tile] * 4, axis=0).T
    count = norms_ref.shape[1] // 8
    for quarter in range(4):

        @pl.when(z % 4 == quarter)
        def _():
            for part in range(count):
                at = quarter * count + part
                value = turned[at : at + 1, :8] + turned[LOW_LANE + at : LOW_LANE + at + 1, :8]
                norms_ref[:, 8 * part : 8 * part + 8] = value


def regroup(owner, near, far):
    matrices, half = near.shape[1:3]
    columns = near.shape[3] - LANES
    vmem = pl.BlockSpec(memory_space=pltpu.VMEM)
    return pl.pallas_call(
        regroup_kernel,
        in_specs=[pl.BlockSpec(memory_space=pltpu.SMEM), vmem, vmem],
        out_specs=[vmem, vmem],
        out_shape=[
            jax.ShapeDtypeStruct((matrices, 2 * half, columns), BF16),
            jax.ShapeDtypeStruct((1, columns // 16), F32),
        ],
        compiler_params=pltpu.CompilerParams(vmem_limit_bytes=VMEM_LIMIT),
        name="regroup",
    )(owner, near, far)


def move(name, block, axis, pairs):
    with jax.named_scope(name):
        return lax.ppermute(block, axis, pairs)


def on_device(grad, momentum, owner):
    matrices, rows, columns = grad.shape
    core = lax.axis_index("core")
    up = [(i, (i + 1) % 4) for i in range(4)]
    down = [((i + 1) % 4, i) for i in range(4)]
    swap = [(0, 1), (1, 0)]

    new_momentum, halves, send = momentum_step(grad, momentum)
    got = lax.ppermute(send, "core", swap)
    halves = lax.dynamic_update_slice_in_dim(halves, got[None], 1 - core, 0)
    mine = lax.all_to_all(
        halves.reshape(16, rows // 4, columns), "z", split_axis=0, concat_axis=0, tiled=True
    ).reshape(-1, columns)
    other = move("pair", mine, "z", [(i, i ^ 1) for i in range(16)])
    mine_left = move("mine_left", mine, "y", up)
    mine_right = move("mine_right", mine, "y", down)
    other_left = move("other_left", other, "y", up)
    other_right = move("other_right", other, "y", down)
    mine_far = move("mine_far", mine_left, "y", up)
    other_far = move("other_far", other_right, "y", down)
    first = jnp.concatenate([mine, mine_left], axis=0)
    second = jnp.concatenate([mine_right, mine_far], axis=0)
    third = jnp.concatenate([other, other_left], axis=0)
    part = gram_part(first, second, third, other_right)
    blocks = [first, second, third]
    for at, block in enumerate(blocks):
        held, part = lax.optimization_barrier((block, part))
        blocks[at] = move("swap", held, "core", swap)
    last = move("swap_last", jnp.concatenate([other_right, other_far], axis=0), "core", swap)
    slots = products(first, part, other_far, *blocks, last)
    near = lax.all_to_all(slots, "z", split_axis=0, concat_axis=0, tiled=True)
    near = near.reshape(2, matrices, rows // 2, columns + LANES)
    far = lax.ppermute(near, "core", swap)
    out_update, norms = regroup(owner.reshape(matrices), near, far)
    return new_momentum, out_update, norms


def solution(mesh):
    experts, shards = mesh.devices.shape
    split = Mesh(mesh.devices.reshape(experts // 2, 2, 4, shards // 4), ("x", "core", "y", "z"))
    groups, rows = ("x", "core"), ("y", "z")
    return jax.shard_map(
        on_device,
        mesh=split,
        in_specs=(P(groups, rows, None), P(groups, rows, None), P(groups, None)),
        out_specs=(P(groups, rows, None), P(groups, rows, None), P(groups, rows)),
        check_vma=False,
    )
```

```python
import math

import jax
import jax.numpy as jnp
from jax import lax
from jax.experimental import pallas as pl
from jax.experimental.pallas import tpu as pltpu
from jax.sharding import Mesh, PartitionSpec as P

DECAY = 0.95
COEF_A = 3.4445
COEF_B = -4.775
COEF_C = 2.0315
EPSILON = 1e-07

F32 = jnp.float32
BF16 = jnp.bfloat16
VMEM_LIMIT = 36 * 1024 * 1024
LANES = 128
STRIP = 256
LOW_LANE = 64


def momentum_kernel(grad_ref, momentum_ref, new_ref, keep_ref, send_ref):
    core = lax.axis_index("core")
    new = DECAY * momentum_ref[...] + grad_ref[...].astype(F32)
    new_ref[...] = new
    half = send_ref.shape[1]
    first = core == 0
    keep_ref[core] = jnp.where(first, new[:, :half], new[:, half:]).astype(BF16)
    send_ref[...] = jnp.where(first, new[:, half:], new[:, :half]).astype(BF16)


def momentum_step(grad, momentum):
    matrices, rows, columns = grad.shape
    vmem = pl.BlockSpec(memory_space=pltpu.VMEM)
    half = (matrices, rows // 2, columns)
    return pl.pallas_call(
        momentum_kernel,
        in_specs=[vmem, vmem],
        out_specs=[vmem, vmem, vmem],
        out_shape=[
            jax.ShapeDtypeStruct(grad.shape, F32),
            jax.ShapeDtypeStruct((2,) + half, BF16),
            jax.ShapeDtypeStruct(half, BF16),
        ],
        compiler_params=pltpu.CompilerParams(vmem_limit_bytes=60 * 1024 * 1024),
        name="momentum_step",
    )(grad, momentum)


def strips(columns):
    return [(at, min(STRIP, columns - at)) for at in range(0, columns, STRIP)]


def gram_strip(x_ref, at, size):
    return lax.dot_general(
        x_ref[:, at : at + size],
        x_ref[:, at:],
        (((0,), (0,)), ((), ())),
        preferred_element_type=F32,
    )


def gram_sum(refs, at, size):
    total = gram_strip(refs[0], at, size)
    for ref in refs[1:]:
        total = total + gram_strip(ref, at, size)
    return total


def gram_part_kernel(*refs):
    part_ref = refs[-1]
    for at, size in strips(part_ref.shape[1]):
        part_ref[at : at + size, at:] = gram_sum(refs[:-1], at, size)


def gram_part(*blocks):
    rows, columns = sum(block.shape[0] for block in blocks), blocks[0].shape[1]
    vmem = pl.BlockSpec(memory_space=pltpu.VMEM)
    return pl.pallas_call(
        gram_part_kernel,
        in_specs=[vmem] * len(blocks),
        out_specs=vmem,
        out_shape=jax.ShapeDtypeStruct((columns, columns), F32),
        compiler_params=pltpu.CompilerParams(vmem_limit_bytes=24 * 1024 * 1024),
        cost_estimate=pl.CostEstimate(
            flops=2 * rows * columns * columns, bytes_accessed=0, transcendentals=0
        ),
        name="gram_part",
    )(*blocks)


def times(block, matrix):
    return jnp.dot(block, matrix, preferred_element_type=F32)


def mirror(matrix_ref, cuts, index):
    at, size = cuts[index]
    for low, count in cuts[index + 1 :]:
        matrix_ref[low : low + count, at : at + size] = matrix_ref[
            at : at + size, low : low + count
        ].T


def products_kernel(mine_ref, part_ref, *refs):
    slots_ref, gram_ref, poly_ref = refs[-3:]
    core, b = lax.axis_index("core"), lax.axis_index("z") % 2
    columns = mine_ref.shape[1]
    own_rows = slots_ref.shape[0] * slots_ref.shape[1]
    total_rows = 16 * own_rows
    cuts = strips(columns)
    squares = jnp.zeros((1, 1), F32)
    for index, (at, size) in enumerate(cuts):
        piece = part_ref[at : at + size, at:] + gram_sum(refs[:-3], at, size)
        row = lax.broadcasted_iota(jnp.int32, (size, size), 0)
        column = lax.broadcasted_iota(jnp.int32, (size, size), 1)
        diagonal = jnp.where(row == column, piece[:, :size], 0.0)
        squares = squares + jnp.sum(diagonal, keepdims=True)
        gram_ref[at : at + size, at:] = piece.astype(BF16)
        mirror(gram_ref, cuts, index)
    scale = 0.5 * math.sqrt(columns) / (jnp.sqrt(squares) + EPSILON)
    scale_squared = scale * scale
    for index, (at, size) in enumerate(cuts):
        rows = gram_ref[at : at + size, :]
        square = scale_squared * times(rows, gram_ref[:, at:])
        poly = scale_squared * (COEF_B * rows[:, at:].astype(F32) + COEF_C * square)
        poly_ref[at : at + size, at:] = poly.astype(BF16)
        mirror(poly_ref, cuts, index)
    own = mine_ref[:own_rows, :]
    ortho = COEF_A * own.astype(F32) + times(own, poly_ref[...])
    update = (math.sqrt(total_rows) * scale) * ortho
    slots_ref[:, :, :columns] = update.reshape(16, -1, columns).astype(BF16)

    width = columns // 4
    start = pl.multiple_of(width * (core * 2 + b), 16)
    block = pl.ds(start, width)
    row = lax.broadcasted_iota(jnp.int32, (width, columns), 0)
    column = lax.broadcasted_iota(jnp.int32, (width, columns), 1)
    cross = COEF_A * gram_ref[block, :].astype(F32) + times(poly_ref[block, :], gram_ref[...])
    cross = (scale_squared * cross).astype(BF16)
    resid = COEF_A * cross.astype(F32) + times(cross, poly_ref[...])
    resid = resid - (column == row + start).astype(F32)
    norms = jnp.sqrt(jnp.sum(resid * resid, axis=1, keepdims=True))
    high = norms.astype(BF16).astype(F32)
    low = norms - high
    lane = lax.broadcasted_iota(jnp.int32, (8, LANES), 1)
    extra = jnp.zeros((8, LANES), F32)
    for part in range(width // 8):
        cut = slice(8 * part, 8 * part + 8)
        extra = jnp.where(lane == part, high[cut], extra)
        extra = jnp.where(lane == LOW_LANE + part, low[cut], extra)
    slots_ref[:, :, columns:] = jnp.broadcast_to(extra[None], (16, 8, LANES)).astype(BF16)


def products(mine, part, *blocks):
    columns = mine.shape[1]
    vmem = pl.BlockSpec(memory_space=pltpu.VMEM)
    return pl.pallas_call(
        products_kernel,
        in_specs=[vmem] * (2 + len(blocks)),
        out_specs=vmem,
        out_shape=jax.ShapeDtypeStruct((16, 8, columns + LANES), BF16),
        scratch_shapes=[pltpu.VMEM((columns, columns), BF16)] * 2,
        compiler_params=pltpu.CompilerParams(vmem_limit_bytes=VMEM_LIMIT),
        cost_estimate=pl.CostEstimate(
            flops=12 * 512 * columns * columns, bytes_accessed=0, transcendentals=0
        ),
        name="products",
    )(mine, part, *blocks)


def regroup_kernel(owner_ref, near_ref, far_ref, update_ref, norms_ref):
    core, y, z = lax.axis_index("core"), lax.axis_index("y"), lax.axis_index("z")
    matrices, rows, columns = update_ref.shape
    half = rows // 2
    near, far = near_ref[core], far_ref[core]
    update_ref[:, :half] = jnp.where(core == 0, near, far)[:, :, :columns]
    update_ref[:, half:] = jnp.where(core == 0, far, near)[:, :, :columns]
    near, far = near[:, :, columns:].astype(F32), far[:, :, columns:].astype(F32)
    tiles = jnp.where(z // 8 == core, near, far)
    tiles = jnp.where(z // 4 % 2 == 0, tiles[:, :8], tiles[:, 8:])
    tile = tiles[0]
    for m in range(1, matrices):
        tile = jnp.where(owner_ref[m] == y, tiles[m], tile)
    turned = jnp.concatenate([tile] * 4, axis=0).T
    count = norms_ref.shape[1] // 8
    for quarter in range(4):

        @pl.when(z % 4 == quarter)
        def _():
            for part in range(count):
                at = quarter * count + part
                value = turned[at : at + 1, :8] + turned[LOW_LANE + at : LOW_LANE + at + 1, :8]
                norms_ref[:, 8 * part : 8 * part + 8] = value


def regroup(owner, near, far):
    matrices, half = near.shape[1:3]
    columns = near.shape[3] - LANES
    vmem = pl.BlockSpec(memory_space=pltpu.VMEM)
    return pl.pallas_call(
        regroup_kernel,
        in_specs=[pl.BlockSpec(memory_space=pltpu.SMEM), vmem, vmem],
        out_specs=[vmem, vmem],
        out_shape=[
            jax.ShapeDtypeStruct((matrices, 2 * half, columns), BF16),
            jax.ShapeDtypeStruct((1, columns // 16), F32),
        ],
        compiler_params=pltpu.CompilerParams(vmem_limit_bytes=VMEM_LIMIT),
        name="regroup",
    )(owner, near, far)


def move(name, block, axis, pairs):
    with jax.named_scope(name):
        return lax.ppermute(block, axis, pairs)


def on_device(grad, momentum, owner):
    matrices, rows, columns = grad.shape
    core = lax.axis_index("core")
    up = [(i, (i + 1) % 4) for i in range(4)]
    down = [((i + 1) % 4, i) for i in range(4)]
    pairs = [(i, i ^ 1) for i in range(16)]
    swap = [(0, 1), (1, 0)]

    new_momentum, halves, send = momentum_step(grad, momentum)
    got = lax.ppermute(send, "core", swap)
    halves = lax.dynamic_update_slice_in_dim(halves, got[None], 1 - core, 0)
    mine = lax.all_to_all(
        halves.reshape(16, rows // 4, columns), "z", split_axis=0, concat_axis=0, tiled=True
    ).reshape(-1, columns)
    other = move("pair", mine, "z", pairs)
    mine_left = move("mine_left", mine, "y", up)
    mine_right = move("mine_right", mine, "y", down)
    mine_far = move("mine_far", mine_left, "y", up)
    other_right = move("other_right", other, "y", down)
    other_left = move("pair_left", mine_left, "z", pairs)
    other_far = move("pair_far", mine_far, "z", pairs)
    mine = jnp.concatenate([mine, mine_left, mine_right, mine_far], axis=0)
    mine_swapped = move("swap_mine", mine, "core", swap)
    other = jnp.concatenate([other, other_left, other_right, other_far], axis=0)
    other_swapped = move("swap_other", other, "core", swap)
    part = gram_part(mine, mine_swapped)
    slots = products(mine, part, other, other_swapped)
    near = lax.all_to_all(slots, "z", split_axis=0, concat_axis=0, tiled=True)
    near = near.reshape(2, matrices, rows // 2, columns + LANES)
    far = lax.ppermute(near, "core", swap)
    out_update, norms = regroup(owner.reshape(matrices), near, far)
    return new_momentum, out_update, norms


def solution(mesh):
    experts, shards = mesh.devices.shape
    split = Mesh(mesh.devices.reshape(experts // 2, 2, 4, shards // 4), ("x", "core", "y", "z"))
    groups, rows = ("x", "core"), ("y", "z")
    return jax.shard_map(
        on_device,
        mesh=split,
        in_specs=(P(groups, rows, None), P(groups, rows, None), P(groups, None)),
        out_specs=(P(groups, rows, None), P(groups, rows, None), P(groups, rows)),
        check_vma=False,
    )
```

```python
import functools
import math

import jax
import jax.numpy as jnp
from jax import lax
from jax.experimental import pallas as pl
from jax.experimental.pallas import tpu as pltpu
from jax.sharding import Mesh, PartitionSpec as P

DECAY = 0.95
COEF_A = 3.4445
COEF_B = -4.775
COEF_C = 2.0315
EPSILON = 1e-07

F32 = jnp.float32
BF16 = jnp.bfloat16
VMEM_LIMIT = 36 * 1024 * 1024
LANES = 128
STRIP = 256
LOW_LANE = 64


def momentum_kernel(grad_ref, momentum_ref, new_ref, keep_ref, send_ref):
    core = lax.axis_index("core")
    new = DECAY * momentum_ref[...] + grad_ref[...].astype(F32)
    new_ref[...] = new
    half = send_ref.shape[1]
    first = core == 0
    keep_ref[core] = jnp.where(first, new[:, :half], new[:, half:]).astype(BF16)
    send_ref[...] = jnp.where(first, new[:, half:], new[:, :half]).astype(BF16)


def momentum_step(grad, momentum):
    matrices, rows, columns = grad.shape
    vmem = pl.BlockSpec(memory_space=pltpu.VMEM)
    half = (matrices, rows // 2, columns)
    return pl.pallas_call(
        momentum_kernel,
        in_specs=[vmem, vmem],
        out_specs=[vmem, vmem, vmem],
        out_shape=[
            jax.ShapeDtypeStruct(grad.shape, F32),
            jax.ShapeDtypeStruct((2,) + half, BF16),
            jax.ShapeDtypeStruct(half, BF16),
        ],
        compiler_params=pltpu.CompilerParams(vmem_limit_bytes=60 * 1024 * 1024),
        name="momentum_step",
    )(grad, momentum)


def strips(columns):
    return [(at, min(STRIP, columns - at)) for at in range(0, columns, STRIP)]


def gram_strip(x_ref, at, size):
    return lax.dot_general(
        x_ref[:, at : at + size],
        x_ref[:, at:],
        (((0,), (0,)), ((), ())),
        preferred_element_type=F32,
    )


def gram_sum(refs, at, size):
    total = gram_strip(refs[0], at, size)
    for ref in refs[1:]:
        total = total + gram_strip(ref, at, size)
    return total


def gram_part_kernel(more, *refs):
    part_ref = refs[-1]
    for at, size in strips(part_ref.shape[1]):
        total = gram_sum(refs[more:-1], at, size)
        if more:
            total = total + refs[0][at : at + size, at:]
        part_ref[at : at + size, at:] = total


def gram_part(part, *blocks):
    given = () if part is None else (part,)
    rows, columns = sum(block.shape[0] for block in blocks), blocks[0].shape[1]
    vmem = pl.BlockSpec(memory_space=pltpu.VMEM)
    return pl.pallas_call(
        functools.partial(gram_part_kernel, len(given)),
        in_specs=[vmem] * (len(given) + len(blocks)),
        out_specs=vmem,
        out_shape=jax.ShapeDtypeStruct((columns, columns), F32),
        compiler_params=pltpu.CompilerParams(vmem_limit_bytes=24 * 1024 * 1024),
        cost_estimate=pl.CostEstimate(
            flops=2 * rows * columns * columns, bytes_accessed=0, transcendentals=0
        ),
        name="gram_part",
    )(*given, *blocks)


def times(block, matrix):
    return jnp.dot(block, matrix, preferred_element_type=F32)


def mirror(matrix_ref, cuts, index):
    at, size = cuts[index]
    for low, count in cuts[index + 1 :]:
        matrix_ref[low : low + count, at : at + size] = matrix_ref[
            at : at + size, low : low + count
        ].T


def products_kernel(mine_ref, part_ref, *refs):
    slots_ref, gram_ref, poly_ref = refs[-3:]
    core, b = lax.axis_index("core"), lax.axis_index("z") % 2
    columns = mine_ref.shape[1]
    own_rows = slots_ref.shape[0] * slots_ref.shape[1]
    total_rows = 16 * own_rows
    cuts = strips(columns)
    squares = jnp.zeros((1, 1), F32)
    for index, (at, size) in enumerate(cuts):
        piece = part_ref[at : at + size, at:] + gram_sum(refs[:-3], at, size)
        row = lax.broadcasted_iota(jnp.int32, (size, size), 0)
        column = lax.broadcasted_iota(jnp.int32, (size, size), 1)
        diagonal = jnp.where(row == column, piece[:, :size], 0.0)
        squares = squares + jnp.sum(diagonal, keepdims=True)
        gram_ref[at : at + size, at:] = piece.astype(BF16)
        mirror(gram_ref, cuts, index)
    scale = 0.5 * math.sqrt(columns) / (jnp.sqrt(squares) + EPSILON)
    scale_squared = scale * scale
    for index, (at, size) in enumerate(cuts):
        rows = gram_ref[at : at + size, :]
        square = scale_squared * times(rows, gram_ref[:, at:])
        poly = scale_squared * (COEF_B * rows[:, at:].astype(F32) + COEF_C * square)
        poly_ref[at : at + size, at:] = poly.astype(BF16)
        mirror(poly_ref, cuts, index)
    own = mine_ref[:own_rows, :]
    ortho = COEF_A * own.astype(F32) + times(own, poly_ref[...])
    update = (math.sqrt(total_rows) * scale) * ortho
    slots_ref[:, :, :columns] = update.reshape(16, -1, columns).astype(BF16)

    width = columns // 4
    start = pl.multiple_of(width * (core * 2 + b), 16)
    block = pl.ds(start, width)
    row = lax.broadcasted_iota(jnp.int32, (width, columns), 0)
    column = lax.broadcasted_iota(jnp.int32, (width, columns), 1)
    cross = COEF_A * gram_ref[block, :].astype(F32) + times(poly_ref[block, :], gram_ref[...])
    cross = (scale_squared * cross).astype(BF16)
    resid = COEF_A * cross.astype(F32) + times(cross, poly_ref[...])
    resid = resid - (column == row + start).astype(F32)
    norms = jnp.sqrt(jnp.sum(resid * resid, axis=1, keepdims=True))
    high = norms.astype(BF16).astype(F32)
    low = norms - high
    lane = lax.broadcasted_iota(jnp.int32, (8, LANES), 1)
    extra = jnp.zeros((8, LANES), F32)
    for part in range(width // 8):
        cut = slice(8 * part, 8 * part + 8)
        extra = jnp.where(lane == part, high[cut], extra)
        extra = jnp.where(lane == LOW_LANE + part, low[cut], extra)
    slots_ref[:, :, columns:] = jnp.broadcast_to(extra[None], (16, 8, LANES)).astype(BF16)


def products(mine, part, *blocks):
    columns = mine.shape[1]
    vmem = pl.BlockSpec(memory_space=pltpu.VMEM)
    return pl.pallas_call(
        products_kernel,
        in_specs=[vmem] * (2 + len(blocks)),
        out_specs=vmem,
        out_shape=jax.ShapeDtypeStruct((16, 8, columns + LANES), BF16),
        scratch_shapes=[pltpu.VMEM((columns, columns), BF16)] * 2,
        compiler_params=pltpu.CompilerParams(vmem_limit_bytes=VMEM_LIMIT),
        cost_estimate=pl.CostEstimate(
            flops=12 * 512 * columns * columns, bytes_accessed=0, transcendentals=0
        ),
        name="products",
    )(mine, part, *blocks)


def regroup_kernel(owner_ref, near_ref, far_ref, update_ref, norms_ref):
    core, y, z = lax.axis_index("core"), lax.axis_index("y"), lax.axis_index("z")
    matrices, rows, columns = update_ref.shape
    half = rows // 2
    near, far = near_ref[core], far_ref[core]
    update_ref[:, :half] = jnp.where(core == 0, near, far)[:, :, :columns]
    update_ref[:, half:] = jnp.where(core == 0, far, near)[:, :, :columns]
    near, far = near[:, :, columns:].astype(F32), far[:, :, columns:].astype(F32)
    tiles = jnp.where(z // 8 == core, near, far)
    tiles = jnp.where(z // 4 % 2 == 0, tiles[:, :8], tiles[:, 8:])
    tile = tiles[0]
    for m in range(1, matrices):
        tile = jnp.where(owner_ref[m] == y, tiles[m], tile)
    turned = jnp.concatenate([tile] * 4, axis=0).T
    count = norms_ref.shape[1] // 8
    for quarter in range(4):

        @pl.when(z % 4 == quarter)
        def _():
            for part in range(count):
                at = quarter * count + part
                value = turned[at : at + 1, :8] + turned[LOW_LANE + at : LOW_LANE + at + 1, :8]
                norms_ref[:, 8 * part : 8 * part + 8] = value


def regroup(owner, near, far):
    matrices, half = near.shape[1:3]
    columns = near.shape[3] - LANES
    vmem = pl.BlockSpec(memory_space=pltpu.VMEM)
    return pl.pallas_call(
        regroup_kernel,
        in_specs=[pl.BlockSpec(memory_space=pltpu.SMEM), vmem, vmem],
        out_specs=[vmem, vmem],
        out_shape=[
            jax.ShapeDtypeStruct((matrices, 2 * half, columns), BF16),
            jax.ShapeDtypeStruct((1, columns // 16), F32),
        ],
        compiler_params=pltpu.CompilerParams(vmem_limit_bytes=VMEM_LIMIT),
        name="regroup",
    )(owner, near, far)


def move(name, block, axis, pairs):
    with jax.named_scope(name):
        return lax.ppermute(block, axis, pairs)


def on_device(grad, momentum, owner):
    matrices, rows, columns = grad.shape
    core = lax.axis_index("core")
    up = [(i, (i + 1) % 4) for i in range(4)]
    down = [((i + 1) % 4, i) for i in range(4)]
    pairs = [(i, i ^ 1) for i in range(16)]
    swap = [(0, 1), (1, 0)]

    new_momentum, halves, send = momentum_step(grad, momentum)
    got = lax.ppermute(send, "core", swap)
    halves = lax.dynamic_update_slice_in_dim(halves, got[None], 1 - core, 0)
    mine = lax.all_to_all(
        halves.reshape(16, rows // 4, columns), "z", split_axis=0, concat_axis=0, tiled=True
    ).reshape(-1, columns)
    other = move("pair", mine, "z", pairs)
    mine_left = move("mine_left", mine, "y", up)
    mine_right = move("mine_right", mine, "y", down)
    mine_far = move("mine_far", mine_left, "y", up)
    other_right = move("other_right", other, "y", down)
    other_left = move("pair_left", mine_left, "z", pairs)
    other_far = move("pair_far", mine_far, "z", pairs)
    mine = jnp.concatenate([mine, mine_left, mine_right, mine_far], axis=0)
    mine_swapped = move("swap_mine", mine, "core", swap)
    other = jnp.concatenate([other, other_left, other_right, other_far], axis=0)
    part = gram_part(None, mine)
    held, part = lax.optimization_barrier((other, part))
    other_swapped = move("swap_other", held, "core", swap)
    part = gram_part(part, other, mine_swapped)
    slots = products(mine, part, other_swapped)
    near = lax.all_to_all(slots, "z", split_axis=0, concat_axis=0, tiled=True)
    near = near.reshape(2, matrices, rows // 2, columns + LANES)
    far = lax.ppermute(near, "core", swap)
    out_update, norms = regroup(owner.reshape(matrices), near, far)
    return new_momentum, out_update, norms


def solution(mesh):
    experts, shards = mesh.devices.shape
    split = Mesh(mesh.devices.reshape(experts // 2, 2, 4, shards // 4), ("x", "core", "y", "z"))
    groups, rows = ("x", "core"), ("y", "z")
    return jax.shard_map(
        on_device,
        mesh=split,
        in_specs=(P(groups, rows, None), P(groups, rows, None), P(groups, None)),
        out_specs=(P(groups, rows, None), P(groups, rows, None), P(groups, rows)),
        check_vma=False,
    )
```

```python
import functools
import math

import jax
import jax.numpy as jnp
from jax import lax
from jax.experimental import pallas as pl
from jax.experimental.pallas import tpu as pltpu
from jax.sharding import Mesh, PartitionSpec as P

DECAY = 0.95
COEF_A = 3.4445
COEF_B = -4.775
COEF_C = 2.0315
EPSILON = 1e-07

F32 = jnp.float32
BF16 = jnp.bfloat16
VMEM_LIMIT = 36 * 1024 * 1024
LANES = 128
STRIP = 256
LOW_LANE = 64


def momentum_kernel(grad_ref, momentum_ref, new_ref, keep_ref, send_ref):
    core = lax.axis_index("core")
    new = DECAY * momentum_ref[...] + grad_ref[...].astype(F32)
    new_ref[...] = new
    half = send_ref.shape[1]
    first = core == 0
    keep_ref[core] = jnp.where(first, new[:, :half], new[:, half:]).astype(BF16)
    send_ref[...] = jnp.where(first, new[:, half:], new[:, :half]).astype(BF16)


def momentum_step(grad, momentum):
    matrices, rows, columns = grad.shape
    vmem = pl.BlockSpec(memory_space=pltpu.VMEM)
    half = (matrices, rows // 2, columns)
    return pl.pallas_call(
        momentum_kernel,
        in_specs=[vmem, vmem],
        out_specs=[vmem, vmem, vmem],
        out_shape=[
            jax.ShapeDtypeStruct(grad.shape, F32),
            jax.ShapeDtypeStruct((2,) + half, BF16),
            jax.ShapeDtypeStruct(half, BF16),
        ],
        compiler_params=pltpu.CompilerParams(vmem_limit_bytes=60 * 1024 * 1024),
        name="momentum_step",
    )(grad, momentum)


def strips(columns):
    return [(at, min(STRIP, columns - at)) for at in range(0, columns, STRIP)]


def gram_strip(x_ref, at, size):
    return lax.dot_general(
        x_ref[:, at : at + size],
        x_ref[:, at:],
        (((0,), (0,)), ((), ())),
        preferred_element_type=F32,
    )


def gram_sum(refs, at, size):
    total = gram_strip(refs[0], at, size)
    for ref in refs[1:]:
        total = total + gram_strip(ref, at, size)
    return total


def gram_part_kernel(more, *refs):
    part_ref = refs[-1]
    for at, size in strips(part_ref.shape[1]):
        total = gram_sum(refs[more:-1], at, size)
        if more:
            total = total + refs[0][at : at + size, at:]
        part_ref[at : at + size, at:] = total


def gram_part(part, *blocks):
    given = () if part is None else (part,)
    rows, columns = sum(block.shape[0] for block in blocks), blocks[0].shape[1]
    vmem = pl.BlockSpec(memory_space=pltpu.VMEM)
    return pl.pallas_call(
        functools.partial(gram_part_kernel, len(given)),
        in_specs=[vmem] * (len(given) + len(blocks)),
        out_specs=vmem,
        out_shape=jax.ShapeDtypeStruct((columns, columns), F32),
        compiler_params=pltpu.CompilerParams(vmem_limit_bytes=24 * 1024 * 1024),
        cost_estimate=pl.CostEstimate(
            flops=2 * rows * columns * columns, bytes_accessed=0, transcendentals=0
        ),
        name="gram_part",
    )(*given, *blocks)


def times(block, matrix):
    return jnp.dot(block, matrix, preferred_element_type=F32)


def mirror(matrix_ref, cuts, index):
    at, size = cuts[index]
    for low, count in cuts[index + 1 :]:
        matrix_ref[low : low + count, at : at + size] = matrix_ref[
            at : at + size, low : low + count
        ].T


def products_kernel(mine_ref, part_ref, *refs):
    slots_ref, gram_ref, poly_ref = refs[-3:]
    core, b = lax.axis_index("core"), lax.axis_index("z") % 2
    columns = mine_ref.shape[1]
    own_rows = slots_ref.shape[0] * slots_ref.shape[1]
    total_rows = 16 * own_rows
    cuts = strips(columns)
    squares = jnp.zeros((1, 1), F32)
    for index, (at, size) in enumerate(cuts):
        piece = part_ref[at : at + size, at:] + gram_sum(refs[:-3], at, size)
        row = lax.broadcasted_iota(jnp.int32, (size, size), 0)
        column = lax.broadcasted_iota(jnp.int32, (size, size), 1)
        diagonal = jnp.where(row == column, piece[:, :size], 0.0)
        squares = squares + jnp.sum(diagonal, keepdims=True)
        gram_ref[at : at + size, at:] = piece.astype(BF16)
        mirror(gram_ref, cuts, index)
    scale = 0.5 * math.sqrt(columns) / (jnp.sqrt(squares) + EPSILON)
    scale_squared = scale * scale
    for index, (at, size) in enumerate(cuts):
        rows = gram_ref[at : at + size, :]
        square = scale_squared * times(rows, gram_ref[:, at:])
        poly = scale_squared * (COEF_B * rows[:, at:].astype(F32) + COEF_C * square)
        poly_ref[at : at + size, at:] = poly.astype(BF16)
        mirror(poly_ref, cuts, index)
    own = mine_ref[:own_rows, :]
    ortho = COEF_A * own.astype(F32) + times(own, poly_ref[...])
    update = (math.sqrt(total_rows) * scale) * ortho
    slots_ref[:, :, :columns] = update.reshape(16, -1, columns).astype(BF16)

    width = columns // 4
    start = pl.multiple_of(width * (core * 2 + b), 16)
    block = pl.ds(start, width)
    row = lax.broadcasted_iota(jnp.int32, (width, columns), 0)
    column = lax.broadcasted_iota(jnp.int32, (width, columns), 1)
    cross = COEF_A * gram_ref[block, :].astype(F32) + times(poly_ref[block, :], gram_ref[...])
    cross = (scale_squared * cross).astype(BF16)
    resid = COEF_A * cross.astype(F32) + times(cross, poly_ref[...])
    resid = resid - (column == row + start).astype(F32)
    norms = jnp.sqrt(jnp.sum(resid * resid, axis=1, keepdims=True))
    high = norms.astype(BF16).astype(F32)
    low = norms - high
    lane = lax.broadcasted_iota(jnp.int32, (8, LANES), 1)
    extra = jnp.zeros((8, LANES), F32)
    for part in range(width // 8):
        cut = slice(8 * part, 8 * part + 8)
        extra = jnp.where(lane == part, high[cut], extra)
        extra = jnp.where(lane == LOW_LANE + part, low[cut], extra)
    slots_ref[:, :, columns:] = jnp.broadcast_to(extra[None], (16, 8, LANES)).astype(BF16)


def products(mine, part, *blocks):
    columns = mine.shape[1]
    vmem = pl.BlockSpec(memory_space=pltpu.VMEM)
    return pl.pallas_call(
        products_kernel,
        in_specs=[vmem] * (2 + len(blocks)),
        out_specs=vmem,
        out_shape=jax.ShapeDtypeStruct((16, 8, columns + LANES), BF16),
        scratch_shapes=[pltpu.VMEM((columns, columns), BF16)] * 2,
        compiler_params=pltpu.CompilerParams(vmem_limit_bytes=VMEM_LIMIT),
        cost_estimate=pl.CostEstimate(
            flops=12 * 512 * columns * columns, bytes_accessed=0, transcendentals=0
        ),
        name="products",
    )(mine, part, *blocks)


def regroup_kernel(owner_ref, near_ref, far_ref, update_ref, norms_ref):
    core, y, z = lax.axis_index("core"), lax.axis_index("y"), lax.axis_index("z")
    matrices, rows, columns = update_ref.shape
    half = rows // 2
    near, far = near_ref[core], far_ref[core]
    update_ref[:, :half] = jnp.where(core == 0, near, far)[:, :, :columns]
    update_ref[:, half:] = jnp.where(core == 0, far, near)[:, :, :columns]
    near, far = near[:, :, columns:].astype(F32), far[:, :, columns:].astype(F32)
    tiles = jnp.where(z // 8 == core, near, far)
    tiles = jnp.where(z // 4 % 2 == 0, tiles[:, :8], tiles[:, 8:])
    tile = tiles[0]
    for m in range(1, matrices):
        tile = jnp.where(owner_ref[m] == y, tiles[m], tile)
    turned = jnp.concatenate([tile] * 4, axis=0).T
    count = norms_ref.shape[1] // 8
    for quarter in range(4):

        @pl.when(z % 4 == quarter)
        def _():
            for part in range(count):
                at = quarter * count + part
                value = turned[at : at + 1, :8] + turned[LOW_LANE + at : LOW_LANE + at + 1, :8]
                norms_ref[:, 8 * part : 8 * part + 8] = value


def regroup(owner, near, far):
    matrices, half = near.shape[1:3]
    columns = near.shape[3] - LANES
    vmem = pl.BlockSpec(memory_space=pltpu.VMEM)
    return pl.pallas_call(
        regroup_kernel,
        in_specs=[pl.BlockSpec(memory_space=pltpu.SMEM), vmem, vmem],
        out_specs=[vmem, vmem],
        out_shape=[
            jax.ShapeDtypeStruct((matrices, 2 * half, columns), BF16),
            jax.ShapeDtypeStruct((1, columns // 16), F32),
        ],
        compiler_params=pltpu.CompilerParams(vmem_limit_bytes=VMEM_LIMIT),
        name="regroup",
    )(owner, near, far)


def move(name, block, axis, pairs):
    with jax.named_scope(name):
        return lax.ppermute(block, axis, pairs)


def on_device(grad, momentum, owner):
    matrices, rows, columns = grad.shape
    core = lax.axis_index("core")
    up = [(i, (i + 1) % 4) for i in range(4)]
    down = [((i + 1) % 4, i) for i in range(4)]
    pairs = [(i, i ^ 1) for i in range(16)]
    swap = [(0, 1), (1, 0)]

    new_momentum, halves, send = momentum_step(grad, momentum)
    got = lax.ppermute(send, "core", swap)
    halves = lax.dynamic_update_slice_in_dim(halves, got[None], 1 - core, 0)
    mine = lax.all_to_all(
        halves.reshape(16, rows // 4, columns), "z", split_axis=0, concat_axis=0, tiled=True
    ).reshape(-1, columns)
    other = move("pair", mine, "z", pairs)
    mine_left = move("mine_left", mine, "y", up)
    mine_right = move("mine_right", mine, "y", down)
    mine_far = move("mine_far", mine_left, "y", up)
    other_right = move("other_right", other, "y", down)
    other_left = move("pair_left", mine_left, "z", pairs)
    other_far = move("pair_far", mine_far, "z", pairs)
    mine = jnp.concatenate([mine, mine_left, mine_right, mine_far], axis=0)
    other_first = other
    other = jnp.concatenate([other, other_left, other_right, other_far], axis=0)
    part = gram_part(None, mine, other_left)
    mine, part = lax.optimization_barrier((mine, part))
    mine_swapped = move("swap_mine", mine, "core", swap)
    held, part = lax.optimization_barrier((other, part))
    other_swapped = move("swap_other", held, "core", swap)
    part = gram_part(part, other_right, other_first, other_far, mine_swapped)
    slots = products(mine, part, other_swapped)
    near = lax.all_to_all(slots, "z", split_axis=0, concat_axis=0, tiled=True)
    near = near.reshape(2, matrices, rows // 2, columns + LANES)
    far = lax.ppermute(near, "core", swap)
    out_update, norms = regroup(owner.reshape(matrices), near, far)
    return new_momentum, out_update, norms


def solution(mesh):
    experts, shards = mesh.devices.shape
    split = Mesh(mesh.devices.reshape(experts // 2, 2, 4, shards // 4), ("x", "core", "y", "z"))
    groups, rows = ("x", "core"), ("y", "z")
    return jax.shard_map(
        on_device,
        mesh=split,
        in_specs=(P(groups, rows, None), P(groups, rows, None), P(groups, None)),
        out_specs=(P(groups, rows, None), P(groups, rows, None), P(groups, rows)),
        check_vma=False,
    )
```

```python
import functools
import math

import jax
import jax.numpy as jnp
from jax import lax
from jax.experimental import pallas as pl
from jax.experimental.pallas import tpu as pltpu
from jax.sharding import Mesh, PartitionSpec as P

DECAY = 0.95
COEF_A = 3.4445
COEF_B = -4.775
COEF_C = 2.0315
EPSILON = 1e-07

F32 = jnp.float32
BF16 = jnp.bfloat16
VMEM_LIMIT = 36 * 1024 * 1024
LANES = 128
STRIP = 256
LOW_LANE = 64


def momentum_kernel(grad_ref, momentum_ref, new_ref, keep_ref, send_ref):
    core = lax.axis_index("core")
    new = DECAY * momentum_ref[...] + grad_ref[...].astype(F32)
    new_ref[...] = new
    half = send_ref.shape[1]
    first = core == 0
    keep_ref[core] = jnp.where(first, new[:, :half], new[:, half:]).astype(BF16)
    send_ref[...] = jnp.where(first, new[:, half:], new[:, :half]).astype(BF16)


def momentum_step(grad, momentum):
    matrices, rows, columns = grad.shape
    vmem = pl.BlockSpec(memory_space=pltpu.VMEM)
    half = (matrices, rows // 2, columns)
    return pl.pallas_call(
        momentum_kernel,
        in_specs=[vmem, vmem],
        out_specs=[vmem, vmem, vmem],
        out_shape=[
            jax.ShapeDtypeStruct(grad.shape, F32),
            jax.ShapeDtypeStruct((2,) + half, BF16),
            jax.ShapeDtypeStruct(half, BF16),
        ],
        compiler_params=pltpu.CompilerParams(vmem_limit_bytes=60 * 1024 * 1024),
        name="momentum_step",
    )(grad, momentum)


def strips(columns):
    return [(at, min(STRIP, columns - at)) for at in range(0, columns, STRIP)]


def gram_strip(x_ref, at, size):
    return lax.dot_general(
        x_ref[:, at : at + size],
        x_ref[:, at:],
        (((0,), (0,)), ((), ())),
        preferred_element_type=F32,
    )


def gram_sum(refs, at, size):
    total = gram_strip(refs[0], at, size)
    for ref in refs[1:]:
        total = total + gram_strip(ref, at, size)
    return total


def gram_part_kernel(more, *refs):
    part_ref = refs[-1]
    for at, size in strips(part_ref.shape[1]):
        total = gram_sum(refs[more:-1], at, size)
        if more:
            total = total + refs[0][at : at + size, at:]
        part_ref[at : at + size, at:] = total


def gram_part(part, *blocks):
    given = () if part is None else (part,)
    rows, columns = sum(block.shape[0] for block in blocks), blocks[0].shape[1]
    vmem = pl.BlockSpec(memory_space=pltpu.VMEM)
    return pl.pallas_call(
        functools.partial(gram_part_kernel, len(given)),
        in_specs=[vmem] * (len(given) + len(blocks)),
        out_specs=vmem,
        out_shape=jax.ShapeDtypeStruct((columns, columns), F32),
        compiler_params=pltpu.CompilerParams(vmem_limit_bytes=24 * 1024 * 1024),
        cost_estimate=pl.CostEstimate(
            flops=2 * rows * columns * columns, bytes_accessed=0, transcendentals=0
        ),
        name="gram_part",
    )(*given, *blocks)


def times(block, matrix):
    return jnp.dot(block, matrix, preferred_element_type=F32)


def mirror(matrix_ref, cuts, index):
    at, size = cuts[index]
    for low, count in cuts[index + 1 :]:
        matrix_ref[low : low + count, at : at + size] = matrix_ref[
            at : at + size, low : low + count
        ].T


def products_kernel(mine_ref, part_ref, *refs):
    slots_ref, gram_ref, poly_ref = refs[-3:]
    core, b = lax.axis_index("core"), lax.axis_index("z") % 2
    columns = mine_ref.shape[1]
    own_rows = slots_ref.shape[0] * slots_ref.shape[1]
    total_rows = 16 * own_rows
    cuts = strips(columns)
    squares = jnp.zeros((1, 1), F32)
    for index, (at, size) in enumerate(cuts):
        piece = part_ref[at : at + size, at:] + gram_sum(refs[:-3], at, size)
        row = lax.broadcasted_iota(jnp.int32, (size, size), 0)
        column = lax.broadcasted_iota(jnp.int32, (size, size), 1)
        diagonal = jnp.where(row == column, piece[:, :size], 0.0)
        squares = squares + jnp.sum(diagonal, keepdims=True)
        gram_ref[at : at + size, at:] = piece.astype(BF16)
        mirror(gram_ref, cuts, index)
    scale = 0.5 * math.sqrt(columns) / (jnp.sqrt(squares) + EPSILON)
    scale_squared = scale * scale
    for index, (at, size) in enumerate(cuts):
        rows = gram_ref[at : at + size, :]
        square = scale_squared * times(rows, gram_ref[:, at:])
        poly = scale_squared * (COEF_B * rows[:, at:].astype(F32) + COEF_C * square)
        poly_ref[at : at + size, at:] = poly.astype(BF16)
        mirror(poly_ref, cuts, index)
    own = mine_ref[:own_rows, :]
    ortho = COEF_A * own.astype(F32) + times(own, poly_ref[...])
    update = (math.sqrt(total_rows) * scale) * ortho
    slots_ref[:, :, :columns] = update.reshape(16, -1, columns).astype(BF16)

    width = columns // 4
    start = pl.multiple_of(width * (core * 2 + b), 16)
    block = pl.ds(start, width)
    row = lax.broadcasted_iota(jnp.int32, (width, columns), 0)
    column = lax.broadcasted_iota(jnp.int32, (width, columns), 1)
    cross = COEF_A * gram_ref[block, :].astype(F32) + times(poly_ref[block, :], gram_ref[...])
    cross = (scale_squared * cross).astype(BF16)
    resid = COEF_A * cross.astype(F32) + times(cross, poly_ref[...])
    resid = resid - (column == row + start).astype(F32)
    norms = jnp.sqrt(jnp.sum(resid * resid, axis=1, keepdims=True))
    high = norms.astype(BF16).astype(F32)
    low = norms - high
    lane = lax.broadcasted_iota(jnp.int32, (8, LANES), 1)
    extra = jnp.zeros((8, LANES), F32)
    for part in range(width // 8):
        cut = slice(8 * part, 8 * part + 8)
        extra = jnp.where(lane == part, high[cut], extra)
        extra = jnp.where(lane == LOW_LANE + part, low[cut], extra)
    slots_ref[:, :, columns:] = jnp.broadcast_to(extra[None], (16, 8, LANES)).astype(BF16)


def products(mine, part, *blocks):
    columns = mine.shape[1]
    vmem = pl.BlockSpec(memory_space=pltpu.VMEM)
    return pl.pallas_call(
        products_kernel,
        in_specs=[vmem] * (2 + len(blocks)),
        out_specs=vmem,
        out_shape=jax.ShapeDtypeStruct((16, 8, columns + LANES), BF16),
        scratch_shapes=[pltpu.VMEM((columns, columns), BF16)] * 2,
        compiler_params=pltpu.CompilerParams(vmem_limit_bytes=VMEM_LIMIT),
        cost_estimate=pl.CostEstimate(
            flops=12 * 512 * columns * columns, bytes_accessed=0, transcendentals=0
        ),
        name="products",
    )(mine, part, *blocks)


def regroup_kernel(owner_ref, near_ref, far_ref, update_ref, norms_ref):
    core, y, z = lax.axis_index("core"), lax.axis_index("y"), lax.axis_index("z")
    matrices, rows, columns = update_ref.shape
    half = rows // 2
    near, far = near_ref[core], far_ref[core]
    update_ref[:, :half] = jnp.where(core == 0, near, far)[:, :, :columns]
    update_ref[:, half:] = jnp.where(core == 0, far, near)[:, :, :columns]
    near, far = near[:, :, columns:].astype(F32), far[:, :, columns:].astype(F32)
    tiles = jnp.where(z // 8 == core, near, far)
    tiles = jnp.where(z // 4 % 2 == 0, tiles[:, :8], tiles[:, 8:])
    tile = tiles[0]
    for m in range(1, matrices):
        tile = jnp.where(owner_ref[m] == y, tiles[m], tile)
    turned = jnp.concatenate([tile] * 4, axis=0).T
    count = norms_ref.shape[1] // 8
    for quarter in range(4):

        @pl.when(z % 4 == quarter)
        def _():
            for part in range(count):
                at = quarter * count + part
                value = turned[at : at + 1, :8] + turned[LOW_LANE + at : LOW_LANE + at + 1, :8]
                norms_ref[:, 8 * part : 8 * part + 8] = value


def regroup(owner, near, far):
    matrices, half = near.shape[1:3]
    columns = near.shape[3] - LANES
    vmem = pl.BlockSpec(memory_space=pltpu.VMEM)
    return pl.pallas_call(
        regroup_kernel,
        in_specs=[pl.BlockSpec(memory_space=pltpu.SMEM), vmem, vmem],
        out_specs=[vmem, vmem],
        out_shape=[
            jax.ShapeDtypeStruct((matrices, 2 * half, columns), BF16),
            jax.ShapeDtypeStruct((1, columns // 16), F32),
        ],
        compiler_params=pltpu.CompilerParams(vmem_limit_bytes=VMEM_LIMIT),
        name="regroup",
    )(owner, near, far)


def move(name, block, axis, pairs):
    with jax.named_scope(name):
        return lax.ppermute(block, axis, pairs)


def on_device(grad, momentum, owner):
    matrices, rows, columns = grad.shape
    core = lax.axis_index("core")
    up = [(i, (i + 1) % 4) for i in range(4)]
    down = [((i + 1) % 4, i) for i in range(4)]
    pairs = [(i, i ^ 1) for i in range(16)]
    swap = [(0, 1), (1, 0)]

    new_momentum, halves, send = momentum_step(grad, momentum)
    got = lax.ppermute(send, "core", swap)
    halves = lax.dynamic_update_slice_in_dim(halves, got[None], 1 - core, 0)
    mine = lax.all_to_all(
        halves.reshape(16, rows // 4, columns), "z", split_axis=0, concat_axis=0, tiled=True
    ).reshape(-1, columns)
    other = move("pair", mine, "z", pairs)
    mine_left = move("mine_left", mine, "y", up)
    mine_right = move("mine_right", mine, "y", down)
    mine_far = move("mine_far", mine_left, "y", up)
    other_right = move("other_right", other, "y", down)
    other_left = move("pair_left", mine_left, "z", pairs)
    other_far = move("pair_far", mine_far, "z", pairs)
    mine = jnp.concatenate([mine, mine_left, mine_right, mine_far], axis=0)
    other_first = other
    other = jnp.concatenate([other, other_left, other_right, other_far], axis=0)
    part = gram_part(None, mine, other_first)
    mine, part = lax.optimization_barrier((mine, part))
    mine_swapped = move("swap_mine", mine, "core", swap)
    held, part = lax.optimization_barrier((other, part))
    other_swapped = move("swap_other", held, "core", swap)
    part = gram_part(part, other_right, other_left, other_far, mine_swapped)
    slots = products(mine, part, other_swapped)
    near = lax.all_to_all(slots, "z", split_axis=0, concat_axis=0, tiled=True)
    near = near.reshape(2, matrices, rows // 2, columns + LANES)
    far = lax.ppermute(near, "core", swap)
    out_update, norms = regroup(owner.reshape(matrices), near, far)
    return new_momentum, out_update, norms


def solution(mesh):
    experts, shards = mesh.devices.shape
    split = Mesh(mesh.devices.reshape(experts // 2, 2, 4, shards // 4), ("x", "core", "y", "z"))
    groups, rows = ("x", "core"), ("y", "z")
    return jax.shard_map(
        on_device,
        mesh=split,
        in_specs=(P(groups, rows, None), P(groups, rows, None), P(groups, None)),
        out_specs=(P(groups, rows, None), P(groups, rows, None), P(groups, rows)),
        check_vma=False,
    )
```

```python
import functools
import math

import jax
import jax.numpy as jnp
from jax import lax
from jax.experimental import pallas as pl
from jax.experimental.pallas import tpu as pltpu
from jax.sharding import Mesh, PartitionSpec as P

DECAY = 0.95
COEF_A = 3.4445
COEF_B = -4.775
COEF_C = 2.0315
EPSILON = 1e-07

F32 = jnp.float32
BF16 = jnp.bfloat16
VMEM_LIMIT = 36 * 1024 * 1024
LANES = 128
STRIP = 256
LOW_LANE = 64


def momentum_kernel(grad_ref, momentum_ref, new_ref, keep_ref, send_ref):
    core = lax.axis_index("core")
    new = DECAY * momentum_ref[...] + grad_ref[...].astype(F32)
    new_ref[...] = new
    half = send_ref.shape[1]
    first = core == 0
    keep_ref[core] = jnp.where(first, new[:, :half], new[:, half:]).astype(BF16)
    send_ref[...] = jnp.where(first, new[:, half:], new[:, :half]).astype(BF16)


def momentum_step(grad, momentum):
    matrices, rows, columns = grad.shape
    vmem = pl.BlockSpec(memory_space=pltpu.VMEM)
    half = (matrices, rows // 2, columns)
    return pl.pallas_call(
        momentum_kernel,
        in_specs=[vmem, vmem],
        out_specs=[vmem, vmem, vmem],
        out_shape=[
            jax.ShapeDtypeStruct(grad.shape, F32),
            jax.ShapeDtypeStruct((2,) + half, BF16),
            jax.ShapeDtypeStruct(half, BF16),
        ],
        compiler_params=pltpu.CompilerParams(vmem_limit_bytes=60 * 1024 * 1024),
        name="momentum_step",
    )(grad, momentum)


def strips(columns):
    return [(at, min(STRIP, columns - at)) for at in range(0, columns, STRIP)]


def gram_strip(x_ref, at, size):
    return lax.dot_general(
        x_ref[:, at : at + size],
        x_ref[:, at:],
        (((0,), (0,)), ((), ())),
        preferred_element_type=F32,
    )


def gram_sum(refs, at, size):
    total = gram_strip(refs[0], at, size)
    for ref in refs[1:]:
        total = total + gram_strip(ref, at, size)
    return total


def gram_part_kernel(more, *refs):
    part_ref = refs[-1]
    for at, size in strips(part_ref.shape[1]):
        total = gram_sum(refs[more:-1], at, size)
        if more:
            total = total + refs[0][at : at + size, at:]
        part_ref[at : at + size, at:] = total


def gram_part(part, *blocks):
    given = () if part is None else (part,)
    rows, columns = sum(block.shape[0] for block in blocks), blocks[0].shape[1]
    vmem = pl.BlockSpec(memory_space=pltpu.VMEM)
    return pl.pallas_call(
        functools.partial(gram_part_kernel, len(given)),
        in_specs=[vmem] * (len(given) + len(blocks)),
        out_specs=vmem,
        out_shape=jax.ShapeDtypeStruct((columns, columns), F32),
        compiler_params=pltpu.CompilerParams(vmem_limit_bytes=24 * 1024 * 1024),
        cost_estimate=pl.CostEstimate(
            flops=2 * rows * columns * columns, bytes_accessed=0, transcendentals=0
        ),
        name="gram_part",
    )(*given, *blocks)


def times(block, matrix):
    return jnp.dot(block, matrix, preferred_element_type=F32)


def mirror(matrix_ref, cuts, index):
    at, size = cuts[index]
    for low, count in cuts[index + 1 :]:
        matrix_ref[low : low + count, at : at + size] = matrix_ref[
            at : at + size, low : low + count
        ].T


def products_kernel(mine_ref, part_ref, *refs):
    slots_ref, gram_ref, poly_ref = refs[-3:]
    core, b = lax.axis_index("core"), lax.axis_index("z") % 2
    columns = mine_ref.shape[1]
    own_rows = slots_ref.shape[0] * slots_ref.shape[1]
    total_rows = 16 * own_rows
    cuts = strips(columns)
    squares = jnp.zeros((1, 1), F32)
    for index, (at, size) in enumerate(cuts):
        piece = part_ref[at : at + size, at:] + gram_sum(refs[:-3], at, size)
        row = lax.broadcasted_iota(jnp.int32, (size, size), 0)
        column = lax.broadcasted_iota(jnp.int32, (size, size), 1)
        diagonal = jnp.where(row == column, piece[:, :size], 0.0)
        squares = squares + jnp.sum(diagonal, keepdims=True)
        gram_ref[at : at + size, at:] = piece.astype(BF16)
        mirror(gram_ref, cuts, index)
    scale = 0.5 * math.sqrt(columns) / (jnp.sqrt(squares) + EPSILON)
    scale_squared = scale * scale
    for index, (at, size) in enumerate(cuts):
        rows = gram_ref[at : at + size, :]
        square = scale_squared * times(rows, gram_ref[:, at:])
        poly = scale_squared * (COEF_B * rows[:, at:].astype(F32) + COEF_C * square)
        poly_ref[at : at + size, at:] = poly.astype(BF16)
        mirror(poly_ref, cuts, index)
    own = mine_ref[:own_rows, :]
    ortho = COEF_A * own.astype(F32) + times(own, poly_ref[...])
    update = (math.sqrt(total_rows) * scale) * ortho
    slots_ref[:, :, :columns] = update.reshape(16, -1, columns).astype(BF16)

    width = columns // 4
    start = pl.multiple_of(width * (core * 2 + b), 16)
    block = pl.ds(start, width)
    row = lax.broadcasted_iota(jnp.int32, (width, columns), 0)
    column = lax.broadcasted_iota(jnp.int32, (width, columns), 1)
    cross = COEF_A * gram_ref[block, :].astype(F32) + times(poly_ref[block, :], gram_ref[...])
    cross = (scale_squared * cross).astype(BF16)
    resid = COEF_A * cross.astype(F32) + times(cross, poly_ref[...])
    resid = resid - (column == row + start).astype(F32)
    norms = jnp.sqrt(jnp.sum(resid * resid, axis=1, keepdims=True))
    high = norms.astype(BF16).astype(F32)
    low = norms - high
    lane = lax.broadcasted_iota(jnp.int32, (8, LANES), 1)
    extra = jnp.zeros((8, LANES), F32)
    for part in range(width // 8):
        cut = slice(8 * part, 8 * part + 8)
        extra = jnp.where(lane == part, high[cut], extra)
        extra = jnp.where(lane == LOW_LANE + part, low[cut], extra)
    slots_ref[:, :, columns:] = jnp.broadcast_to(extra[None], (16, 8, LANES)).astype(BF16)


def products(mine, part, *blocks):
    columns = mine.shape[1]
    vmem = pl.BlockSpec(memory_space=pltpu.VMEM)
    return pl.pallas_call(
        products_kernel,
        in_specs=[vmem] * (2 + len(blocks)),
        out_specs=vmem,
        out_shape=jax.ShapeDtypeStruct((16, 8, columns + LANES), BF16),
        scratch_shapes=[pltpu.VMEM((columns, columns), BF16)] * 2,
        compiler_params=pltpu.CompilerParams(vmem_limit_bytes=VMEM_LIMIT),
        cost_estimate=pl.CostEstimate(
            flops=12 * 512 * columns * columns, bytes_accessed=0, transcendentals=0
        ),
        name="products",
    )(mine, part, *blocks)


def regroup_kernel(owner_ref, near_ref, far_ref, update_ref, norms_ref):
    core, y, z = lax.axis_index("core"), lax.axis_index("y"), lax.axis_index("z")
    matrices, rows, columns = update_ref.shape
    half = rows // 2
    near, far = near_ref[core], far_ref[core]
    update_ref[:, :half] = jnp.where(core == 0, near, far)[:, :, :columns]
    update_ref[:, half:] = jnp.where(core == 0, far, near)[:, :, :columns]
    near, far = near[:, :, columns:].astype(F32), far[:, :, columns:].astype(F32)
    tiles = jnp.where(z // 8 == core, near, far)
    tiles = jnp.where(z // 4 % 2 == 0, tiles[:, :8], tiles[:, 8:])
    tile = tiles[0]
    for m in range(1, matrices):
        tile = jnp.where(owner_ref[m] == y, tiles[m], tile)
    turned = jnp.concatenate([tile] * 4, axis=0).T
    count = norms_ref.shape[1] // 8
    for quarter in range(4):

        @pl.when(z % 4 == quarter)
        def _():
            for part in range(count):
                at = quarter * count + part
                value = turned[at : at + 1, :8] + turned[LOW_LANE + at : LOW_LANE + at + 1, :8]
                norms_ref[:, 8 * part : 8 * part + 8] = value


def regroup(owner, near, far):
    matrices, half = near.shape[1:3]
    columns = near.shape[3] - LANES
    vmem = pl.BlockSpec(memory_space=pltpu.VMEM)
    return pl.pallas_call(
        regroup_kernel,
        in_specs=[pl.BlockSpec(memory_space=pltpu.SMEM), vmem, vmem],
        out_specs=[vmem, vmem],
        out_shape=[
            jax.ShapeDtypeStruct((matrices, 2 * half, columns), BF16),
            jax.ShapeDtypeStruct((1, columns // 16), F32),
        ],
        compiler_params=pltpu.CompilerParams(vmem_limit_bytes=VMEM_LIMIT),
        name="regroup",
    )(owner, near, far)


def move(name, block, axis, pairs):
    with jax.named_scope(name):
        return lax.ppermute(block, axis, pairs)


def on_device(grad, momentum, owner):
    matrices, rows, columns = grad.shape
    core = lax.axis_index("core")
    up = [(i, (i + 1) % 4) for i in range(4)]
    down = [((i + 1) % 4, i) for i in range(4)]
    pairs = [(i, i ^ 1) for i in range(16)]
    swap = [(0, 1), (1, 0)]

    new_momentum, halves, send = momentum_step(grad, momentum)
    got = lax.ppermute(send, "core", swap)
    halves = lax.dynamic_update_slice_in_dim(halves, got[None], 1 - core, 0)
    mine = lax.all_to_all(
        halves.reshape(16, rows // 4, columns), "z", split_axis=0, concat_axis=0, tiled=True
    ).reshape(-1, columns)
    other = move("pair", mine, "z", pairs)
    mine_left = move("mine_left", mine, "y", up)
    mine_right = move("mine_right", mine, "y", down)
    mine_far = move("mine_far", mine_left, "y", up)
    other_right = move("other_right", other, "y", down)
    other_left = move("pair_left", mine_left, "z", pairs)
    other_far = move("pair_far", mine_far, "z", pairs)
    mine = jnp.concatenate([mine, mine_left, mine_right, mine_far], axis=0)
    other_first = other
    other = jnp.concatenate([other, other_left, other_right, other_far], axis=0)
    part = gram_part(None, mine, other_first)
    mine, part = lax.optimization_barrier((mine, part))
    mine_swapped = move("swap_mine", mine, "core", swap)
    part = gram_part(part, other_left, other_right)
    held, part = lax.optimization_barrier((other, part))
    other_swapped = move("swap_other", held, "core", swap)
    part = gram_part(part, other_far, mine_swapped)
    slots = products(mine, part, other_swapped)
    near = lax.all_to_all(slots, "z", split_axis=0, concat_axis=0, tiled=True)
    near = near.reshape(2, matrices, rows // 2, columns + LANES)
    far = lax.ppermute(near, "core", swap)
    out_update, norms = regroup(owner.reshape(matrices), near, far)
    return new_momentum, out_update, norms


def solution(mesh):
    experts, shards = mesh.devices.shape
    split = Mesh(mesh.devices.reshape(experts // 2, 2, 4, shards // 4), ("x", "core", "y", "z"))
    groups, rows = ("x", "core"), ("y", "z")
    return jax.shard_map(
        on_device,
        mesh=split,
        in_specs=(P(groups, rows, None), P(groups, rows, None), P(groups, None)),
        out_specs=(P(groups, rows, None), P(groups, rows, None), P(groups, rows)),
        check_vma=False,
    )
```
